512 devices in a mesh: slab: 64 (over z, x, core), batch: 8 (over y).
Axes of the slice: x: 4, y: 8, z: 8, core: 2. Of those that a mesh axis runs over, the one named last changes fastest.
Arguments:
- features: bfloat16 [8, 256, 512, 128], P('batch', 'slab'), may hold values from -6 to 6
- cotangent: bfloat16 [8, 256, 512, 128], P('batch', 'slab'), may hold values from -6 to 6
- coords: int32 [8, 256], P('batch', 'slab'), may hold values from 0 to 16, as said below
- orientation: int32 [8], P('batch'), may hold values from 0 to 7
- kernel: bfloat16 [27, 128, 128], replicated, may hold values from -0.109375 to 0.109375
Outputs:
- output: bfloat16 [8, 256, 512, 128], P('batch', 'slab')
- input_grad: bfloat16 [8, 256, 512, 128], P('batch', 'slab')
- kernel_grad: float32 [3456, 128], replicated
The draws below stay inside these ranges and needn't reach their ends.
Inputs may be any that keep to these rules, and one draw needn't show every extreme that they name: `coords`: for each volume and slab, its 4 entries list distinct brick positions first and the value 4 * 4 for the empty slots after them; the numbers of listed bricks of slab s and of slab s + 32 of the same volume add up to 4; in every volume some slab lists 4 bricks.
All inputs are finite; a program needn't handle non-finite values.
Results may differ from the reference program's by a relative error of at most 0.001.
Values may be sent and summed in bfloat16 or wider, within the bound.
A program may use at most 128 MiB of HBM per device.

```python
import jax
import jax.numpy as jnp
from jax import lax

C = 128
B = 8
G = 4
SLOTS = 4
N_SLAB = 64
N_BATCH = 8


def draw_coords(key, part):
    key = jax.random.fold_in(key, 11)
    half_axis = N_SLAB // 2
    quota_slots = SLOTS // 2
    key_count, key_full, key_centre, key_jitter, key_ties = jax.random.split(key, 5)
    offsets = jax.random.randint(key_count, (N_BATCH, half_axis), -quota_slots, quota_slots + 1)
    full_slab = jax.random.randint(key_full, (N_BATCH, 1), 0, half_axis)
    offsets = jnp.where(jnp.arange(half_axis)[None, :] == full_slab, quota_slots, offsets)
    counts = quota_slots + jnp.concatenate([offsets, -offsets], axis=1)
    centre = jax.random.randint(key_centre, (N_BATCH, 1, 2), 0, G)
    jitter = jax.random.randint(key_jitter, (N_BATCH, N_SLAB, 2), -1, 2)
    centre = jnp.clip(centre + jitter, 0, G - 1)
    positions = jnp.arange(G * G)
    pos_row = positions // G
    pos_col = positions % G
    distance = (pos_row[None, None, :] - centre[:, :, 0:1]) ** 2 + (pos_col[None, None, :] - centre[:, :, 1:2]) ** 2
    slab_keys = jax.random.split(key_ties, N_BATCH * N_SLAB)
    tie_break = jax.vmap(lambda one_key: jax.random.permutation(one_key, G * G))(slab_keys).reshape(N_BATCH, N_SLAB, G * G)
    ranking = jnp.argsort(distance * (G * G) + tie_break, axis=-1, stable=True)
    slot_index = jnp.arange(SLOTS)
    chosen = jnp.where(slot_index[None, None, :] < counts[:, :, None], ranking[:, :, :SLOTS], G * G)
    return chosen.reshape(N_BATCH, N_SLAB * SLOTS).astype(jnp.int32)


def place_ends(result, own_key, smallest, largest):
    longest = result.shape.index(max(result.shape))
    spots = []
    for shift in (0, 1):
        where = [jax.random.randint(jax.random.fold_in(own_key, axis), (), 0, length) for axis, length in enumerate(result.shape)]
        where[longest] = (where[longest] + shift) % result.shape[longest]
        spots.append(tuple(where))
    return result.at[spots[0]].set(smallest).at[spots[1]].set(largest)


def level_of(own_key, dims, cuts, least, top_value):
    gain = 1.0
    for dim, shards_of in cuts:
        heights = jax.random.uniform(jax.random.fold_in(jax.random.fold_in(own_key, 6), dim), (shards_of,), jnp.float32, least / len(cuts), top_value / len(cuts))
        gain = gain * jnp.repeat(jnp.exp(heights), dims[dim] // shards_of).reshape((-1,) + (1,) * (len(dims) - 1 - dim))
    return gain


def noise(rng, dims, deviation, most, cuts=(), held_as=jnp.bfloat16):
    loudness = level_of(rng, dims, cuts, -0.22, 0.18) if cuts else 1.0
    result = jax.random.normal(rng, dims, jnp.float32) * deviation * loudness
    return jnp.minimum(jnp.maximum(result, -most), most).astype(held_as)


def setup_inputs(seed: int = 0) -> dict:
    key_of = jax.random.split(jax.random.key(seed), 6)
    return {
        "features": noise(key_of[0], (N_BATCH, N_SLAB * SLOTS, B * B * B, C), 1.0, 6.0, ((0, 8), (1, 64))),
        "cotangent": noise(key_of[1], (N_BATCH, N_SLAB * SLOTS, B * B * B, C), 1.0, 6.0, ((0, 8), (1, 64))),
        "coords": draw_coords(jax.random.fold_in(key_of[5], 71), 0),
        "orientation": place_ends(jax.random.randint(key_of[3], (N_BATCH,), 0, 8), jax.random.fold_in(key_of[3], 1), 0, 7).astype(jnp.int32),
        "kernel": noise(key_of[4], (27, C, C), (27 * C) ** -0.5, 0.109375),
    }


def tap_table(flip_code):
    tap_ids = jnp.arange(27, dtype=jnp.int32)
    tap_z = tap_ids // 9
    tap_y = (tap_ids // 3) % 3
    tap_x = tap_ids % 3
    tap_x = jnp.where(flip_code % 2 == 1, 2 - tap_x, tap_x)
    tap_y = jnp.where((flip_code // 2) % 2 == 1, 2 - tap_y, tap_y)
    tap_z = jnp.where((flip_code // 4) % 2 == 1, 2 - tap_z, tap_z)
    return (tap_z * 9 + tap_y * 3 + tap_x).astype(jnp.int32)


def unfold(patches, mirrored):
    brick_side = patches.shape[1] - 2
    channels = patches.shape[-1]
    pieces = []
    for tap_z in range(3):
        for tap_y in range(3):
            for tap_x in range(3):
                if mirrored:
                    start_z, start_y, start_x = 2 - tap_z, 2 - tap_y, 2 - tap_x
                else:
                    start_z, start_y, start_x = tap_z, tap_y, tap_x
                pieces.append(patches[:, start_z:start_z + brick_side, start_y:start_y + brick_side, start_x:start_x + brick_side, :])
    return jnp.concatenate(pieces, axis=-1).reshape(-1, 27 * channels)


def one_volume(features, cotangent, coords, flip_code, kernel):
    channels = kernel.shape[-1]
    active = coords < G * G
    source = jnp.stack([features, cotangent]).astype(jnp.float32).reshape(2, N_SLAB, SLOTS, B, B, B, channels)
    source = jnp.where(active[None, :, :, None, None, None, None], source, 0.0)
    grid_ids = jnp.arange(G, dtype=jnp.int32)[:, None] * G + jnp.arange(G, dtype=jnp.int32)[None, :]
    placing = (coords[:, None, None, :] == grid_ids[None, :, :, None]).astype(jnp.float32)
    volume = jnp.einsum('nyxs,knszqrc->knzyqxrc', placing, source).reshape(2, N_SLAB * B, G * B, G * B, channels)
    padded = jnp.pad(volume, ((0, 0), (1, 1), (1, 1), (1, 1), (0, 0)))
    effective = kernel.astype(jnp.float32)[tap_table(flip_code)]
    forward_flat = effective.reshape(27 * channels, channels)
    backward_flat = jnp.swapaxes(effective, 1, 2).reshape(27 * channels, channels)

    def slab_pass(inputs):
        slab_id, slab_coords = inputs
        clipped = jnp.minimum(slab_coords, G * G - 1).astype(jnp.int32)

        def extract(pos_row, pos_col):
            starts = (jnp.int32(0), (slab_id * B).astype(jnp.int32), (pos_row * B).astype(jnp.int32), (pos_col * B).astype(jnp.int32), jnp.int32(0))
            return lax.dynamic_slice(padded, starts, (2, B + 2, B + 2, B + 2, channels))

        patches = jax.vmap(extract)(clipped // G, clipped % G)
        row_mask = slab_coords < G * G
        x_cols = unfold(patches[:, 0], False)
        g_cols = unfold(patches[:, 1], True)
        cell_mask = jnp.repeat(row_mask, B ** 3)[:, None]
        centre = patches[:, 1, 1:B + 1, 1:B + 1, 1:B + 1, :].reshape(-1, channels)
        centre = jnp.where(cell_mask, centre, 0.0)
        out_y = jnp.where(cell_mask, jnp.dot(x_cols, forward_flat, preferred_element_type=jnp.float32), 0.0)
        out_dx = jnp.where(cell_mask, jnp.dot(g_cols, backward_flat, preferred_element_type=jnp.float32), 0.0)
        kernel_term = lax.dot_general(x_cols, centre, (((0,), (0,)), ((), ())), preferred_element_type=jnp.float32)
        return (out_y.astype(jnp.bfloat16).reshape(SLOTS, B ** 3, channels),
                out_dx.astype(jnp.bfloat16).reshape(SLOTS, B ** 3, channels), kernel_term)

    out_y, out_dx, kernel_terms = lax.map(slab_pass, (jnp.arange(N_SLAB, dtype=jnp.int32), coords))
    summed = jnp.sum(kernel_terms, axis=0).reshape(27, channels, channels)[tap_table(flip_code)]
    return out_y.reshape(N_SLAB * SLOTS, B ** 3, channels), out_dx.reshape(N_SLAB * SLOTS, B ** 3, channels), summed


def reference(features, cotangent, coords, orientation, kernel):
    channels = kernel.shape[-1]

    def run_volume(inputs):
        return one_volume(inputs[0], inputs[1], inputs[2], inputs[3], kernel)

    out_y, out_dx, kernel_terms = lax.map(run_volume, (features, cotangent, coords.reshape(N_BATCH, N_SLAB, SLOTS), orientation))
    grad_scale = float(N_BATCH * N_SLAB * (SLOTS // 2) * B ** 3) ** -0.5
    kernel_grad = (jnp.sum(kernel_terms, axis=0) * grad_scale).reshape(27 * channels, channels)
    return out_y, out_dx, kernel_grad
```

```python
import functools

import jax
import jax.numpy as jnp
from jax import lax
from jax.experimental import pallas as pl
from jax.experimental.pallas import tpu as pltpu
from jax.sharding import PartitionSpec as P

C = 128
SLOTS = 4
CELLS = 512
TAPS = 27
NZ, NX, NY = 8, 4, 8
GROUP = 32
CHUNK = 28
QROWS = CHUNK * GROUP
BITS = 14.95
BF = jnp.bfloat16
F32 = jnp.float32
MESH = pl.DeviceIdType.MESH


def place():
    s = lax.axis_index("slab")
    return s // 8, lax.rem(s // 2, 4), lax.rem(s, 2), lax.axis_index("batch")


def device(z, x, core, y):
    return {"slab": z * 8 + x * 2 + core, "batch": y}


def remote(src, dst, send, recv, where):
    return pltpu.make_async_remote_copy(
        src_ref=src, dst_ref=dst, send_sem=send, recv_sem=recv, device_id=where, device_id_type=MESH
    )


def halo_kernel(feat, cot, coords, hv, hu, hc, send, recv):
    s = lax.axis_index("slab")
    up, down = lax.rem(s + 1, 64), lax.rem(s + 63, 64)
    barrier = pltpu.get_barrier_semaphore()
    for peer in (up, down):
        pl.semaphore_signal(barrier, inc=1, device_id={"slab": peer}, device_id_type=MESH)
    pl.semaphore_wait(barrier, 2)
    copies = []
    for d, (peer, plane) in enumerate(((up, 7), (down, 0))):
        for k, (src, dst) in enumerate(((feat.at[:, plane], hv), (cot.at[:, plane], hu), (coords, hc))):
            copies.append(remote(src, dst.at[d], send.at[d, k], recv.at[d, k], {"slab": peer}))
    for copy in copies:
        copy.start()
    for copy in copies:
        copy.wait()


def halo(feat, cot, coords):
    anywhere = pl.BlockSpec(memory_space=pl.ANY)
    return pl.pallas_call(
        halo_kernel,
        out_shape=[
            jax.ShapeDtypeStruct((2, SLOTS, 64, C), BF),
            jax.ShapeDtypeStruct((2, SLOTS, 64, C), BF),
            jax.ShapeDtypeStruct((2, 8, C), jnp.int32),
        ],
        in_specs=[anywhere] * 3,
        out_specs=[anywhere] * 3,
        scratch_shapes=[pltpu.SemaphoreType.DMA((2, 3)), pltpu.SemaphoreType.DMA((2, 3))],
        compiler_params=pltpu.CompilerParams(collective_id=0, has_side_effects=True),
        name="halo_planes",
    )(feat, cot, coords)


def neighbours(slab_coord, pos):
    row, col = pos // 4, lax.rem(pos, 4)
    slots = {}
    for dy in (-1, 0, 1):
        for dx in (-1, 0, 1):
            y, x = row + dy, col + dx
            inside = (y >= 0) & (y < 4) & (x >= 0) & (x < 4) & (pos < 16)
            wanted = jnp.where(inside, y * 4 + x, 99)
            slot = jnp.int32(SLOTS)
            for k in range(SLOTS):
                slot = jnp.where(slab_coord(k) == wanted, k, slot)
            slots[dy, dx] = slot
    return slots


def build_plane(get, slots, even, odd, i, z):
    lane_x = lax.broadcasted_iota(jnp.int32, (10, 8, C), 1)

    def column(dx):
        middle = get(slots[0, dx], 0, 64).astype(F32).reshape(8, 8, C)
        top = get(slots[-1, dx], 48, 16).astype(F32).reshape(2, 8, C)[1:]
        bottom = get(slots[1, dx], 0, 16).astype(F32).reshape(2, 8, C)[:1]
        return jnp.concatenate([top, middle, bottom], axis=0)

    left, centre, right = column(-1), column(0), column(1)
    before = pltpu.roll(jnp.where(lane_x == 7, left, centre), 1, 1)
    after = pltpu.roll(jnp.where(lane_x == 0, right, centre), 7, 1)
    for d, rows in enumerate((before, centre, after)):
        even[d, i, z] = rows[1:9].reshape(64, C).astype(BF)
        odd[d, i, z] = rows.reshape(80, C).astype(BF)


def shifted(even, odd, tap, flips, brick=None):
    tz, ty, tx = tap // 9, tap // 3 % 3, tap % 3
    flip_x, flip_y, flip_z = flips
    z0 = jnp.where(flip_z, 2 - tz, tz)
    x0 = jnp.where(flip_x, 2 - tx, tx)
    which = slice(None) if brick is None else brick
    count = SLOTS if brick is None else 1
    if ty == 1:
        cells = even[x0, which, pl.ds(z0, 8)]
    else:
        y0 = pl.multiple_of(jnp.where(flip_y, 2 - ty, ty) * 8, 16)
        cells = odd[x0, which, pl.ds(z0, 8), pl.ds(y0, 64)]
    return cells.reshape(count * CELLS, C)


def conv_kernel(
    coords, near_coords, code, feat, cot, kernel, hv, hu, out, dx, grad, V, U, HV, HU, KV, even_v, odd_v, even_u, odd_u, cot_t, sems
):
    loads = [
        pltpu.make_async_copy(feat, V.at[pl.ds(0, SLOTS)], sems.at[0]),
        pltpu.make_async_copy(hv, HV.at[:, pl.ds(0, SLOTS)], sems.at[1]),
        pltpu.make_async_copy(cot, U.at[pl.ds(0, SLOTS)], sems.at[2]),
        pltpu.make_async_copy(hu, HU.at[:, pl.ds(0, SLOTS)], sems.at[3]),
        pltpu.make_async_copy(kernel, KV, sems.at[4]),
    ]
    for load in loads:
        load.start()
    s = lax.axis_index("slab")
    for cells in (V, U):
        cells[SLOTS] = jnp.zeros((8, 64, C), BF)
    for planes in (HV, HU):
        for d in range(2):
            planes[d, SLOTS] = jnp.zeros((64, C), BF)
    flip_code = code[0]
    flips = (lax.rem(flip_code, 2) == 1, lax.rem(flip_code // 2, 2) == 1, lax.rem(flip_code // 4, 2) == 1)
    opposite = tuple(jnp.logical_not(f) for f in flips)

    def coord_of(d):
        if d == 1:
            return lambda k: coords[0, k]
        edge = (s == 0) if d == 0 else (s == 63)
        return lambda k: jnp.where(edge, 16, near_coords[d // 2, 0, k])

    def build(cells, planes, even, odd):
        @pl.loop(0, SLOTS)
        def _(i):
            slots = [neighbours(coord_of(d), coords[0, i]) for d in range(3)]

            @pl.loop(0, 8)
            def _(z):
                build_plane(lambda j, a, n: cells[j, z, pl.ds(a, n), :], slots[1], even, odd, i, z + 1)

            for d, z in ((0, 0), (1, 9)):
                build_plane(lambda j, a, n: planes[d, j, pl.ds(a, n), :], slots[2 * d], even, odd, i, z)

    loads[0].wait()
    loads[1].wait()
    build(V, HV, even_v, odd_v)
    loads[2].wait()
    for i in range(SLOTS):
        cells = jnp.where(coords[0, i] < 16, U[i].reshape(CELLS, C), jnp.zeros((), BF))
        cot_t[:, i * CELLS : (i + 1) * CELLS] = cells.T
    for first in range(0, TAPS, 2):
        taps = range(first, min(first + 2, TAPS))
        cols = jnp.concatenate([shifted(even_v, odd_v, t, flips) for t in taps], axis=1)
        sums = jnp.dot(cot_t[...], cols, preferred_element_type=F32)
        for n, t in enumerate(taps):
            grad[t * C : (t + 1) * C] = sums[:, n * C : (n + 1) * C].T
    grad[TAPS * C :] = jnp.zeros((4 * QROWS - TAPS * C, C), F32)
    loads[3].wait()
    build(U, HU, even_u, odd_u)
    loads[4].wait()

    @pl.loop(0, SLOTS)
    def _(i):
        active = coords[0, i] < 16
        for backward in (False, True):
            total = jnp.zeros((CELLS, C), F32)
            for first in range(0, TAPS, 2):
                taps = range(first, min(first + 2, TAPS))
                if backward:
                    cols = jnp.concatenate([shifted(even_u, odd_u, t, opposite, i) for t in taps], axis=1)
                    weights = jnp.concatenate([KV[t * C : (t + 1) * C] for t in taps], axis=1)
                    dims = (((1,), (1,)), ((), ()))
                else:
                    cols = jnp.concatenate([shifted(even_v, odd_v, t, flips, i) for t in taps], axis=1)
                    weights = KV[first * C : (first + len(taps)) * C]
                    dims = (((1,), (0,)), ((), ()))
                total += lax.dot_general(cols, weights, dims, preferred_element_type=F32)
            (dx if backward else out)[i] = jnp.where(active, total, 0.0).astype(BF).reshape(8, 64, C)


def convolve(coords, near_coords, code, feat, cot, kernel, hv, hu):
    smem, vmem = pl.BlockSpec(memory_space=pltpu.SMEM), pl.BlockSpec(memory_space=pltpu.VMEM)
    anywhere = pl.BlockSpec(memory_space=pl.ANY)
    cells, planes = pltpu.VMEM((SLOTS + 1, 8, 64, C), BF), pltpu.VMEM((2, SLOTS + 1, 64, C), BF)
    even, odd = pltpu.VMEM((3, SLOTS, 10, 64, C), BF), pltpu.VMEM((3, SLOTS, 10, 80, C), BF)
    return pl.pallas_call(
        conv_kernel,
        out_shape=[
            jax.ShapeDtypeStruct((SLOTS, 8, 64, C), BF),
            jax.ShapeDtypeStruct((SLOTS, 8, 64, C), BF),
            jax.ShapeDtypeStruct((4 * QROWS, C), F32),
        ],
        in_specs=[smem] * 3 + [anywhere] * 5,
        out_specs=[vmem] * 3,
        scratch_shapes=[cells, cells, planes, planes, pltpu.VMEM((TAPS * C, C), BF), even, odd, even, odd]
        + [pltpu.VMEM((C, SLOTS * CELLS), BF), pltpu.SemaphoreType.DMA((5,))],
        compiler_params=pltpu.CompilerParams(vmem_limit_bytes=48 << 20),
        name="brick_convs",
    )(coords, near_coords, code, feat, cot, kernel, hv, hu)


def encode(rows):
    index = lax.broadcasted_iota(jnp.int32, (32, C), 0)
    top = jnp.max(jnp.where(index < CHUNK, jnp.abs(rows), 0.0), axis=0, keepdims=True)
    power = jnp.ceil(jnp.log2(jnp.maximum(top, 2.0**-100)))
    codes = jnp.round(rows * jnp.exp2(BITS - power))
    codes = jnp.where(index < CHUNK, codes, jnp.broadcast_to(power, (32, C)))
    return codes.astype(jnp.int32).astype(jnp.int16)


def decode(codes):
    values = codes.astype(jnp.int32).astype(F32)
    return values * jnp.exp2(values[CHUNK : CHUNK + 1] - BITS)


def sum_kernel(grad, gathered, own, sibling, out_codes, in_codes, mid_codes, mid_in, sems, core_send, core_recv, s1, r1, s2, r2, s3, r3):
    z, x, core, y = place()
    me = (x * 8 + y, x * 8 + z)
    ring_me = (z, y)

    def group_device(part, j):
        if part == 0:
            return device(z, j // 8, core, lax.rem(j, 8))
        return device(lax.rem(j, 8), j // 8, core, y)

    def ring_device(part, j):
        return device(j, x, core, y) if part == 0 else device(z, x, core, j)

    other = device(z, x, 1 - core, y)
    barrier = pltpu.get_barrier_semaphore()
    pl.semaphore_signal(barrier, inc=1, device_id=other, device_id_type=MESH)
    for part in range(2):

        @pl.loop(1, GROUP)
        def _(k):
            peer = group_device(part, lax.rem(me[part] + k, GROUP))
            pl.semaphore_signal(barrier, inc=1, device_id=peer, device_id_type=MESH)

    pl.semaphore_wait(barrier, 1 + 2 * (GROUP - 1))

    core_copies, loads = [], []
    for part in range(2):
        theirs, mine = (2 * part + 1 - core) * QROWS, (2 * part + core) * QROWS
        core_copies.append(
            remote(
                grad.at[pl.ds(pl.multiple_of(theirs, 8), QROWS)],
                sibling.at[part, pl.ds(0, QROWS)],
                core_send.at[part],
                core_recv.at[part],
                other,
            )
        )
        loads.append(
            pltpu.make_async_copy(
                grad.at[pl.ds(pl.multiple_of(mine, 8), QROWS)], own.at[part, pl.ds(0, QROWS)], sems.at[part]
            )
        )
    for copy in core_copies + loads:
        copy.start()

    def scatter(part, k):
        j = lax.rem(me[part] + k, GROUP)
        return remote(
            out_codes.at[part, j],
            in_codes.at[part, me[part]],
            s1.at[part, j],
            r1.at[part, me[part]],
            group_device(part, j),
        )

    for part in range(2):
        loads[part].wait()
        core_copies[part].wait_recv()

        @pl.loop(0, GROUP // 2)
        def _(pair):
            base = pl.multiple_of(pair * 2 * CHUNK, 8)
            both = own[part, pl.ds(base, 64)] + sibling[part, pl.ds(base, 64)]
            out_codes[part, 2 * pair] = encode(both[:32])
            out_codes[part, 2 * pair + 1] = encode(both[CHUNK : CHUNK + 32])

        @pl.loop(1, GROUP)
        def _(k):
            scatter(part, k).start()

    def exchange(part, k):
        j = lax.rem(ring_me[part] + k, 8)
        return remote(
            mid_codes.at[part],
            mid_in.at[part, ring_me[part]],
            s2.at[part, j],
            r2.at[part, ring_me[part]],
            ring_device(part, j),
        )

    for part in range(2):

        def add(k, total):
            j = lax.rem(me[part] + k, GROUP)
            remote(
                out_codes.at[part, j], in_codes.at[part, j], s1.at[part, j], r1.at[part, j], group_device(part, j)
            ).wait_recv()
            return total + decode(in_codes[part, j])

        total = lax.fori_loop(1, GROUP, add, decode(out_codes[part, me[part]]))
        codes = encode(total)
        mid_codes[part] = codes
        mid_in[part, ring_me[part]] = codes

        @pl.loop(1, 8)
        def _(k):
            exchange(part, k).start()

    def publish(part, k):
        j = lax.rem(me[part] + k, GROUP)
        block = gathered.at[2 * part + core, me[part]]
        return remote(block, block, s3.at[part, j], r3.at[part, me[part]], group_device(part, j))

    for part in range(2):

        @pl.loop(1, 8)
        def _(k):
            j = lax.rem(ring_me[part] + k, 8)
            remote(
                mid_codes.at[part], mid_in.at[part, j], s2.at[part, j], r2.at[part, j], ring_device(part, j)
            ).wait_recv()

        total = decode(mid_in[part, 0])
        for j in range(1, 8):
            total += decode(mid_in[part, j])
        gathered[2 * part + core, me[part]] = encode(total)

        @pl.loop(1, GROUP)
        def _(k):
            publish(part, k).start()

    handed = []
    for part in range(2):

        @pl.loop(1, GROUP)
        def _(k):
            j = lax.rem(me[part] + k, GROUP)
            block = gathered.at[2 * part + core, j]
            remote(block, block, s3.at[part, j], r3.at[part, j], group_device(part, j)).wait_recv()

        block = gathered.at[2 * part + core]
        handed.append(remote(block, block, core_send.at[2 + part], core_recv.at[2 + part], other))
        handed[part].start()

    for part in range(2):
        core_copies[part].wait_send()

        @pl.loop(1, GROUP)
        def _(k):
            scatter(part, k).wait_send()
            publish(part, k).wait_send()

        @pl.loop(1, 8)
        def _(k):
            exchange(part, k).wait_send()

    for part in range(2):
        handed[part].wait_send()
        block = gathered.at[2 * part + 1 - core]
        remote(block, block, core_send.at[2 + part], core_recv.at[2 + part], other).wait_recv()


def sum_codes(grad):
    anywhere, vmem = pl.BlockSpec(memory_space=pl.ANY), pl.BlockSpec(memory_space=pltpu.VMEM)
    dma = pltpu.SemaphoreType.DMA
    return pl.pallas_call(
        sum_kernel,
        out_shape=jax.ShapeDtypeStruct((4, GROUP, 32, C), jnp.int16),
        in_specs=[anywhere],
        out_specs=vmem,
        scratch_shapes=[
            pltpu.VMEM((2, QROWS + 8, C), F32),
            pltpu.VMEM((2, QROWS + 8, C), F32),
            pltpu.VMEM((2, GROUP, 32, C), jnp.int16),
            pltpu.VMEM((2, GROUP, 32, C), jnp.int16),
            pltpu.VMEM((2, 32, C), jnp.int16),
            pltpu.VMEM((2, 8, 32, C), jnp.int16),
            dma((2,)),
            dma((4,)),
            dma((4,)),
            dma((2, GROUP)),
            dma((2, GROUP)),
            dma((2, 8)),
            dma((2, 8)),
            dma((2, GROUP)),
            dma((2, GROUP)),
        ],
        compiler_params=pltpu.CompilerParams(collective_id=1, has_side_effects=True, vmem_limit_bytes=32 << 20),
        name="sum_gradient",
    )(grad)


def decode_kernel(scale, codes, out):
    for q in range(4):

        @pl.loop(0, GROUP // 2 if q < 3 else 13)
        def _(pair):
            low = decode(codes[q, 2 * pair])[:CHUNK]
            high = decode(codes[q, 2 * pair + 1])[:CHUNK]
            start = pl.multiple_of(q * QROWS + pair * 2 * CHUNK, 8)
            out[pl.ds(start, 2 * CHUNK)] = jnp.concatenate([low, high], axis=0) * scale

    tail = jnp.concatenate([decode(codes[3, 26])[:CHUNK], decode(codes[3, 27])[:CHUNK]], axis=0) * scale
    out[pl.ds(3 * QROWS + 26 * CHUNK, 40)] = tail[:40]


def decode_all(codes, scale):
    vmem = pl.BlockSpec(memory_space=pltpu.VMEM)
    return pl.pallas_call(
        functools.partial(decode_kernel, scale),
        out_shape=jax.ShapeDtypeStruct((TAPS * C, C), F32),
        in_specs=[vmem],
        out_specs=vmem,
        compiler_params=pltpu.CompilerParams(vmem_limit_bytes=32 << 20),
        name="decode_gradient",
    )(codes)


def shards(features, cotangent, coords, orientation, kernel):
    feat = features.reshape(SLOTS, 8, 64, C)
    cot = cotangent.reshape(SLOTS, 8, 64, C)
    row = jnp.broadcast_to(jnp.pad(coords, ((0, 0), (0, C - SLOTS))), (8, C))
    hv, hu, hc = halo(feat, cot, row)
    out, dx, grad = convolve(coords, hc, orientation, feat, cot, kernel.reshape(TAPS * C, C), hv, hu)
    scale = float(8 * 64 * 2 * 512) ** -0.5
    total = decode_all(sum_codes(grad), scale)
    shape = (1, SLOTS, CELLS, C)
    return out.reshape(shape), dx.reshape(shape), total


def solution(mesh):
    in_specs = (
        P("batch", "slab", None, None),
        P("batch", "slab", None, None),
        P("batch", "slab"),
        P("batch"),
        P(),
    )
    out_specs = (P("batch", "slab", None, None), P("batch", "slab", None, None), P())
    return jax.shard_map(shards, mesh=mesh, in_specs=in_specs, out_specs=out_specs, check_vma=False)
```

```python
import functools

import jax
import jax.numpy as jnp
from jax import lax
from jax.experimental import pallas as pl
from jax.experimental.pallas import tpu as pltpu
from jax.sharding import PartitionSpec as P

C = 128
SLOTS = 4
CELLS = 512
TAPS = 27
GROUP = 32
PARTS = 4
PART_TAPS = 7
CHUNK = PART_TAPS * C // 2 // GROUP
ROWS = 16
BITS = 14.95
MIDDLE, LOW, HIGH = list(range(9, 18)), list(range(9)), list(range(18, 27))
ORDER = [list(range(9, 16)), [16, 17, 0, 1, 2, 3, 4], [5, 6, 7, 8, 18, 19, 20], list(range(21, 27))]
BF = jnp.bfloat16
F32 = jnp.float32
MESH = pl.DeviceIdType.MESH


def place():
    s = lax.axis_index("slab")
    return s // 8, lax.rem(s // 2, 4), lax.rem(s, 2), lax.axis_index("batch")


def device(z, x, core, y):
    return {"slab": z * 8 + x * 2 + core, "batch": y}


def remote(src, dst, send, recv, where):
    return pltpu.make_async_remote_copy(
        src_ref=src, dst_ref=dst, send_sem=send, recv_sem=recv, device_id=where, device_id_type=MESH
    )


def neighbours(slab_coord, pos):
    row, col = pos // 4, lax.rem(pos, 4)
    slots = {}
    for dy in (-1, 0, 1):
        for dx in (-1, 0, 1):
            y, x = row + dy, col + dx
            inside = (y >= 0) & (y < 4) & (x >= 0) & (x < 4) & (pos < 16)
            wanted = jnp.where(inside, y * 4 + x, 99)
            slot = jnp.int32(SLOTS)
            for k in range(SLOTS):
                slot = jnp.where(slab_coord(k) == wanted, k, slot)
            slots[dy, dx] = slot
    return slots


def build_plane(get, slots, even, odd, i, z):
    lane_x = lax.broadcasted_iota(jnp.int32, (10, 8, C), 1)

    def column(dx):
        middle = get(slots[0, dx], 0, 64).astype(F32).reshape(8, 8, C)
        top = get(slots[-1, dx], 48, 16).astype(F32).reshape(2, 8, C)[1:]
        bottom = get(slots[1, dx], 0, 16).astype(F32).reshape(2, 8, C)[:1]
        return jnp.concatenate([top, middle, bottom], axis=0)

    left, centre, right = column(-1), column(0), column(1)
    before = pltpu.roll(jnp.where(lane_x == 7, left, centre), 1, 1)
    after = pltpu.roll(jnp.where(lane_x == 0, right, centre), 7, 1)
    for d, rows in enumerate((before, centre, after)):
        even[d, i, z] = rows[1:9].reshape(64, C).astype(BF)
        odd[d, i, z] = rows.reshape(80, C).astype(BF)


def shifted(even, odd, tap, brick=None):
    tz, ty, tx = tap // 9, tap // 3 % 3, tap % 3
    which = slice(None) if brick is None else brick
    count = SLOTS if brick is None else 1
    if ty == 1:
        cells = even[tx, which, tz : tz + 8]
    else:
        cells = odd[tx, which, tz : tz + 8, 8 * ty : 8 * ty + 64]
    return cells.reshape(count * CELLS, C)


def encode(rows):
    index = lax.broadcasted_iota(jnp.int32, (ROWS, C), 0)
    top = jnp.max(jnp.where(index < CHUNK, jnp.abs(rows), 0.0), axis=0, keepdims=True)
    power = jnp.ceil(jnp.log2(jnp.maximum(top, 2.0**-100)))
    codes = jnp.round(rows * jnp.exp2(BITS - power))
    codes = jnp.where(index < CHUNK, codes, jnp.broadcast_to(power, (ROWS, C)))
    return codes.astype(jnp.int32).astype(jnp.int16)


def decode(codes):
    values = codes.astype(jnp.int32).astype(F32)
    return values * jnp.exp2(values[CHUNK : CHUNK + 1] - BITS)


def main_kernel(
    coords, code, feat, cot, kernel, out, dx, gathered,
    V, U, HV, HU, HC, mine_c, near, KV, even_v, odd_v, even_u, odd_u, cot_t, edge_t, terms, grad, sibling,
    out_codes, in_codes, mid_codes, mid_in, OUT, DX,
    load_sem, halo_send, halo_recv, core_send, core_recv, s1, r1, s2, r2, s3, r3, hand_send, hand_recv, store_sem,
):
    slab = lax.axis_index("slab")
    z, x, core, y = place()
    me = (x * 8 + y, x * 8 + z)
    ring_me = (z, y)
    other = device(z, x, 1 - core, y)
    has_lower, has_upper = slab > 0, slab < 63
    lower, upper = {"slab": lax.rem(slab + 63, 64)}, {"slab": lax.rem(slab + 1, 64)}

    def group_device(kind, j):
        if kind == 0:
            return device(z, j // 8, core, lax.rem(j, 8))
        return device(lax.rem(j, 8), j // 8, core, y)

    def ring_device(kind, j):
        return device(j, x, core, y) if kind == 0 else device(z, x, core, j)

    barrier = pltpu.get_barrier_semaphore()
    pl.semaphore_signal(barrier, inc=1, device_id=other, device_id_type=MESH)

    @pl.when(has_upper & (core == 1))
    def _():
        pl.semaphore_signal(barrier, inc=1, device_id=upper, device_id_type=MESH)

    @pl.when(has_lower & (core == 0))
    def _():
        pl.semaphore_signal(barrier, inc=1, device_id=lower, device_id_type=MESH)

    for kind in range(2):

        @pl.loop(1, GROUP)
        def _(k):
            peer = group_device(kind, lax.rem(me[kind] + k, GROUP))
            pl.semaphore_signal(barrier, inc=1, device_id=peer, device_id_type=MESH)

    loads = [
        pltpu.make_async_copy(feat, V.at[pl.ds(0, SLOTS)], load_sem.at[0]),
        pltpu.make_async_copy(cot, U.at[pl.ds(0, SLOTS)], load_sem.at[1]),
        pltpu.make_async_copy(kernel, KV, load_sem.at[2]),
    ]
    for load in loads:
        load.start()
    for cells in (V, U):
        cells[SLOTS] = jnp.zeros((8, 64, C), BF)
    for planes in (HV, HU):
        for d in range(2):
            planes[d, SLOTS] = jnp.zeros((64, C), BF)
    for z0 in (0, 9):
        even_v[:, :, z0] = jnp.zeros((3, SLOTS, 64, C), BF)
        odd_v[:, :, z0] = jnp.zeros((3, SLOTS, 80, C), BF)
    lane = lax.broadcasted_iota(jnp.int32, (8, C), 1)
    row = jnp.full((8, C), 16, jnp.int32)
    for k in range(SLOTS):
        row = jnp.where(lane == k, coords[0, k], row)
    mine_c[...] = row
    flip_code = code[0]
    flip_x, flip_y, flip_z = lax.rem(flip_code, 2), lax.rem(flip_code // 2, 2), lax.rem(flip_code // 4, 2)

    def mirrored(tap):
        tz, ty, tx = tap // 9, tap // 3 % 3, tap % 3
        return tap + flip_z * (18 - 18 * tz) + flip_y * (6 - 6 * ty) + flip_x * (2 - 2 * tx)

    def inner(cells, even, odd):
        @pl.loop(0, SLOTS)
        def _(i):
            slots = neighbours(lambda k: coords[0, k], coords[0, i])

            @pl.loop(0, 8)
            def _(plane):
                build_plane(lambda j, a, n: cells[j, plane, pl.ds(a, n), :], slots, even, odd, i, plane + 1)

    def outer(planes, even, odd):
        @pl.loop(0, SLOTS)
        def _(i):
            for d, plane, there in ((0, 0, has_lower), (1, 9, has_upper)):
                slots = neighbours(lambda k: jnp.where(there, near[d, 0, k], 16), coords[0, i])
                build_plane(lambda j, a, n: planes[d, j, pl.ds(a, n), :], slots, even, odd, i, plane)

    loads[0].wait()
    inner(V, even_v, odd_v)
    loads[1].wait()
    zero = jnp.zeros((), BF)
    for i in range(SLOTS):
        cells = jnp.where(coords[0, i] < 16, U[i].reshape(CELLS, C), zero)
        cot_t[:, i * CELLS : (i + 1) * CELLS] = cells.T
    for d, plane in ((0, 0), (1, 7)):
        edge = [jnp.where(coords[0, i] < 16, U[i, plane], zero) for i in range(SLOTS)]
        edge_t[d] = jnp.concatenate(edge, axis=0).T
    def products(taps, left, read):
        for first in range(0, len(taps), 2):
            two = taps[first : first + 2]
            cols = jnp.concatenate([read(t) for t in two], axis=1)
            sums = jnp.dot(left, cols, preferred_element_type=F32)
            for k, t in enumerate(two):
                yield t, sums[:, k * C : (k + 1) * C].T

    def fill(part):
        for n, t in enumerate(ORDER[part]):
            grad[part, n * C : (n + 1) * C] = terms[mirrored(t)]

    for t, term in products(MIDDLE + LOW + HIGH, cot_t[...], lambda t: shifted(even_v, odd_v, t)):
        terms[t] = term
    fill(0)
    for n in range(len(ORDER[PARTS - 1]), PART_TAPS):
        grad[PARTS - 1, n * C : (n + 1) * C] = jnp.zeros((C, C), F32)

    half = PART_TAPS * C // 2

    def to_core(part):
        src = grad.at[part, pl.ds(pl.multiple_of((1 - core) * half, 8), half)]
        return remote(src, sibling.at[part, pl.ds(0, half)], core_send.at[part], core_recv.at[part], other)

    pl.semaphore_wait(barrier, 2 * GROUP - 1 + ((has_upper & (core == 1)) | (has_lower & (core == 0))).astype(jnp.int32))

    halos = []
    for d, (there, peer, plane) in enumerate(((has_upper, upper, 7), (has_lower, lower, 0))):
        group = [
            remote(mine_c, HC.at[d], halo_send.at[d, 0], halo_recv.at[d, 0], peer),
            remote(feat.at[:, plane], HV.at[d, pl.ds(0, SLOTS)], halo_send.at[d, 1], halo_recv.at[d, 1], peer),
            remote(cot.at[:, plane], HU.at[d, pl.ds(0, SLOTS)], halo_send.at[d, 2], halo_recv.at[d, 2], peer),
        ]
        halos.append((there, group))

    def start_halo(k):
        for there, group in halos:
            pl.when(there)(group[k].start)

    def end_halo(k):
        for (there, _), (_, group) in zip(reversed(halos), halos, strict=True):
            pl.when(there)(group[k].wait_recv)

    start_halo(0)
    start_halo(1)
    to_core(0).start()
    start_halo(2)

    def scatter(part, k):
        kind = part % 2
        j = lax.rem(me[kind] + k, GROUP)
        return remote(
            out_codes.at[part, j], in_codes.at[part, me[kind]], s1.at[part], r1.at[part], group_device(kind, j)
        )

    def send_part(part):
        to_core(part).wait_recv()

        @pl.loop(0, GROUP // 4)
        def _(four):
            base = pl.multiple_of(four * 4 * CHUNK, 8)
            mine = grad[part, pl.ds(pl.multiple_of(core * half + base, 8), 64)]
            rows = mine + sibling[part, pl.ds(base, 64)]
            for n in range(4):
                out_codes[part, 4 * four + n] = encode(rows[n * CHUNK : n * CHUNK + ROWS])

        @pl.loop(1, GROUP)
        def _(k):
            scatter(part, k).start()

    send_part(0)

    end_halo(0)
    near_copy = pltpu.make_async_copy(HC, near, load_sem.at[3])
    near_copy.start()
    end_halo(1)
    near_copy.wait()
    outer(HV, even_v, odd_v)

    def edge_cells(t):
        ty, tx, side = t // 3 % 3, t % 3, 9 * (t // 18)
        if ty == 1:
            return even_v[tx, :, side].reshape(SLOTS * 64, C)
        return odd_v[tx, :, side, 8 * ty : 8 * ty + 64].reshape(SLOTS * 64, C)

    for d, taps in enumerate((LOW, HIGH)):
        for t, term in products(taps, edge_t[d], edge_cells):
            terms[t] += term
    for part in range(1, PARTS):
        fill(part)
        to_core(part).start()
    for part in range(1, PARTS):
        send_part(part)

    def convolve(i, backward):
        total = jnp.zeros((CELLS, C), F32)
        for first in range(0, TAPS, 2):
            taps = range(first, min(first + 2, TAPS))
            if backward:
                cols = jnp.concatenate([shifted(even_u, odd_u, 26 - t, i) for t in taps], axis=1)
                weights = jnp.concatenate([KV[mirrored(t)] for t in taps], axis=1)
                dims = (((1,), (1,)), ((), ()))
            else:
                cols = jnp.concatenate([shifted(even_v, odd_v, t, i) for t in taps], axis=1)
                weights = jnp.concatenate([KV[mirrored(t)] for t in taps], axis=0)
                dims = (((1,), (0,)), ((), ()))
            total += lax.dot_general(cols, weights, dims, preferred_element_type=F32)
        return jnp.where(coords[0, i] < 16, total, 0.0).astype(BF).reshape(8, 64, C)

    loads[2].wait()

    @pl.loop(0, SLOTS)
    def _(i):
        OUT[i] = convolve(i, False)

    out_copy = pltpu.make_async_copy(OUT, out, store_sem.at[0])
    out_copy.start()
    inner(U, even_u, odd_u)
    end_halo(2)
    outer(HU, even_u, odd_u)

    def exchange(part, k):
        kind = part % 2
        j = lax.rem(ring_me[kind] + k, 8)
        return remote(
            mid_codes.at[part], mid_in.at[part, ring_me[kind]], s2.at[part], r2.at[part], ring_device(kind, j)
        )

    def several(buffer, count, send, recv):
        blocks = buffer.at[pl.ds(0, count)]
        return remote(blocks, blocks, send, recv, other)

    for part in range(PARTS):
        kind = part % 2
        several(in_codes.at[part], GROUP - 1, s1.at[part], r1.at[part]).wait_recv()

        def add(k, total):
            return total + decode(in_codes[part, lax.rem(me[kind] + k, GROUP)])

        total = lax.fori_loop(1, GROUP, add, decode(out_codes[part, me[kind]]))
        codes = encode(total)
        mid_codes[part] = codes
        mid_in[part, ring_me[kind]] = codes

        @pl.loop(1, 8)
        def _(k):
            exchange(part, k).start()

    @pl.loop(0, 2)
    def _(i):
        DX[i] = convolve(i, True)

    def publish(part, k):
        kind = part % 2
        block = gathered.at[part, core, me[kind]]
        return remote(block, block, s3.at[part], r3.at[part], group_device(kind, lax.rem(me[kind] + k, GROUP)))

    for part in range(PARTS):
        kind = part % 2
        several(mid_in.at[part], 7, s2.at[part], r2.at[part]).wait_recv()
        total = decode(mid_in[part, 0])
        for j in range(1, 8):
            total += decode(mid_in[part, j])
        gathered[part, core, me[kind]] = encode(total)

        @pl.loop(1, GROUP)
        def _(k):
            publish(part, k).start()

    @pl.loop(2, SLOTS)
    def _(i):
        DX[i] = convolve(i, True)

    dx_copy = pltpu.make_async_copy(DX, dx, store_sem.at[1])
    dx_copy.start()

    def hand(part):
        block = gathered.at[part, core]
        return remote(block, block, hand_send.at[part], hand_recv.at[part], other)

    for part in range(PARTS):
        several(gathered.at[part, core], GROUP - 1, s3.at[part], r3.at[part]).wait_recv()
        hand(part).start()

    for part in range(PARTS):
        to_core(part).wait_send()
        several(out_codes.at[part], GROUP - 1, s1.at[part], r1.at[part]).wait_send()
        several(mid_in.at[part], 7, s2.at[part], r2.at[part]).wait_send()
        several(gathered.at[part, core], GROUP - 1, s3.at[part], r3.at[part]).wait_send()
        hand(part).wait_send()
    for there, group in halos:
        for copy in group:
            pl.when(there)(copy.wait_send)
    out_copy.wait()
    dx_copy.wait()
    for part in range(PARTS):
        hand(part).wait_recv()


def main_call(coords, code, feat, cot, kernel):
    smem, vmem = pl.BlockSpec(memory_space=pltpu.SMEM), pl.BlockSpec(memory_space=pltpu.VMEM)
    anywhere = pl.BlockSpec(memory_space=pl.ANY)
    dma = pltpu.SemaphoreType.DMA
    cells, planes = pltpu.VMEM((SLOTS + 1, 8, 64, C), BF), pltpu.VMEM((2, SLOTS + 1, 64, C), BF)
    even, odd = pltpu.VMEM((3, SLOTS, 10, 64, C), BF), pltpu.VMEM((3, SLOTS, 10, 80, C), BF)
    bricks = pltpu.VMEM((SLOTS, 8, 64, C), BF)
    codes = pltpu.VMEM((PARTS, GROUP, ROWS, C), jnp.int16)
    return pl.pallas_call(
        main_kernel,
        out_shape=[
            jax.ShapeDtypeStruct((SLOTS, 8, 64, C), BF),
            jax.ShapeDtypeStruct((SLOTS, 8, 64, C), BF),
            jax.ShapeDtypeStruct((PARTS, 2, GROUP, ROWS, C), jnp.int16),
        ],
        in_specs=[smem] * 2 + [anywhere] * 3,
        out_specs=[anywhere, anywhere, vmem],
        scratch_shapes=[
            cells, cells, planes, planes, pltpu.VMEM((2, 8, C), jnp.int32), pltpu.VMEM((8, C), jnp.int32),
            pltpu.SMEM((2, 8, C), jnp.int32), pltpu.VMEM((TAPS, C, C), BF), even, odd, even, odd,
            pltpu.VMEM((C, SLOTS * CELLS), BF), pltpu.VMEM((2, C, SLOTS * 64), BF), pltpu.VMEM((TAPS, C, C), F32),
            pltpu.VMEM((PARTS, PART_TAPS * C + 8, C), F32), pltpu.VMEM((PARTS, PART_TAPS * C // 2 + 8, C), F32),
            codes, codes, pltpu.VMEM((PARTS, ROWS, C), jnp.int16), pltpu.VMEM((PARTS, 8, ROWS, C), jnp.int16),
            bricks, bricks,
            dma((4,)), dma((2, 3)), dma((2, 3)), dma((PARTS,)), dma((PARTS,)), dma((PARTS,)), dma((PARTS,)),
            dma((PARTS,)), dma((PARTS,)), dma((PARTS,)), dma((PARTS,)), dma((PARTS,)), dma((PARTS,)), dma((2,)),
        ],
        compiler_params=pltpu.CompilerParams(collective_id=0, has_side_effects=True, vmem_limit_bytes=58 << 20),
        name="brick_convs",
    )(coords, code, feat, cot, kernel)


def result_kernel(scale, out_in, dx_in, codes, out, dx, grad, held, rows, bricks, sems):
    loads = [pltpu.make_async_copy(codes.at[p], held.at[p], sems.at[2 + p]) for p in range(PARTS)]
    passed = [(out_in, out), (dx_in, dx)]
    fetches = [pltpu.make_async_copy(src, bricks.at[k], sems.at[k]) for k, (src, _) in enumerate(passed)]
    copies = [pltpu.make_async_copy(bricks.at[k], dst, sems.at[k]) for k, (_, dst) in enumerate(passed)]
    for load in loads + fetches:
        load.start()
    half = PART_TAPS * C // 2
    stores = []
    for part in range(PARTS):
        if part >= 2:
            fetches[part - 2].wait()
            copies[part - 2].start()
        loads[part].wait()
        for core in range(2):

            @pl.loop(0, GROUP // 4)
            def _(four):
                blocks = [decode(held[part, core, 4 * four + n])[:CHUNK] for n in range(4)]
                start = pl.multiple_of(core * half + four * 4 * CHUNK, 8)
                rows[part, pl.ds(start, 4 * CHUNK)] = jnp.concatenate(blocks, axis=0) * scale

        first = 0
        taps = ORDER[part]
        for n in range(1, len(taps) + 1):
            if n == len(taps) or taps[n] != taps[n - 1] + 1:
                store = pltpu.make_async_copy(
                    rows.at[part, pl.ds(first * C, (n - first) * C)],
                    grad.at[pl.ds(taps[first] * C, (n - first) * C)],
                    sems.at[2 + PARTS + len(stores)],
                )
                store.start()
                stores.append(store)
                first = n
    for copy in stores + copies:
        copy.wait()


def results(out, dx, codes, scale):
    anywhere = pl.BlockSpec(memory_space=pl.ANY)
    return pl.pallas_call(
        functools.partial(result_kernel, scale),
        out_shape=[
            jax.ShapeDtypeStruct((SLOTS, 8, 64, C), BF),
            jax.ShapeDtypeStruct((SLOTS, 8, 64, C), BF),
            jax.ShapeDtypeStruct((TAPS * C, C), F32),
        ],
        in_specs=[anywhere] * 3,
        out_specs=[anywhere] * 3,
        scratch_shapes=[
            pltpu.VMEM((PARTS, 2, GROUP, ROWS, C), jnp.int16),
            pltpu.VMEM((PARTS, PART_TAPS * C, C), F32),
            pltpu.VMEM((2, SLOTS, 8, 64, C), BF),
            pltpu.SemaphoreType.DMA((2 + 4 * PARTS,)),
        ],
        compiler_params=pltpu.CompilerParams(vmem_limit_bytes=58 << 20),
        name="results",
    )(out, dx, codes)


def shards(features, cotangent, coords, orientation, kernel):
    feat = features.reshape(SLOTS, 8, 64, C)
    cot = cotangent.reshape(SLOTS, 8, 64, C)
    out, dx, codes = main_call(coords, orientation, feat, cot, kernel)
    out, dx, total = results(out, dx, codes, float(8 * 64 * 2 * 512) ** -0.5)
    shape = (1, SLOTS, CELLS, C)
    return out.reshape(shape), dx.reshape(shape), total


def solution(mesh):
    in_specs = (
        P("batch", "slab", None, None),
        P("batch", "slab", None, None),
        P("batch", "slab"),
        P("batch"),
        P(),
    )
    out_specs = (P("batch", "slab", None, None), P("batch", "slab", None, None), P())
    return jax.shard_map(shards, mesh=mesh, in_specs=in_specs, out_specs=out_specs, check_vma=False)
```

```python
import functools

import jax
import jax.numpy as jnp
from jax import lax
from jax.experimental import pallas as pl
from jax.experimental.pallas import tpu as pltpu
from jax.sharding import PartitionSpec as P

C = 128
SLOTS = 4
CELLS = 512
TAPS = 27
GROUP = 32
PARTS = 4
PART_TAPS = 7
CHUNK = PART_TAPS * C // 2 // GROUP
ROWS = 16
BITS = 14.95
MIDDLE, LOW, HIGH = list(range(9, 18)), list(range(9)), list(range(18, 27))
ORDER = [list(range(9, 16)), [16, 17, 0, 1, 2, 3, 4], [5, 6, 7, 8, 18, 19, 20], list(range(21, 27))]
BF = jnp.bfloat16
F32 = jnp.float32
MESH = pl.DeviceIdType.MESH


def place():
    s = lax.axis_index("slab")
    return s // 8, (s // 2) & 3, s & 1, lax.axis_index("batch")


def device(z, x, core, y):
    return {"slab": z * 8 + x * 2 + core, "batch": y}


def remote(src, dst, send, recv, where):
    return pltpu.make_async_remote_copy(
        src_ref=src, dst_ref=dst, send_sem=send, recv_sem=recv, device_id=where, device_id_type=MESH
    )


def neighbours(slab_coord, pos):
    row, col = pos >> 2, pos & 3
    slots = {}
    for dy in (-1, 0, 1):
        for dx in (-1, 0, 1):
            y, x = row + dy, col + dx
            inside = (y >= 0) & (y < 4) & (x >= 0) & (x < 4) & (pos < 16)
            wanted = jnp.where(inside, y * 4 + x, 99)
            slot = jnp.int32(SLOTS)
            for k in range(SLOTS):
                slot = jnp.where(slab_coord(k) == wanted, k, slot)
            slots[dy, dx] = slot
    return slots


def build_plane(get, slots, even, odd, i, z):
    lane_x = lax.broadcasted_iota(jnp.int32, (10, 8, C), 1)

    def column(dx):
        middle = get(slots[0, dx], 0, 64).astype(F32).reshape(8, 8, C)
        top = get(slots[-1, dx], 48, 16).astype(F32).reshape(2, 8, C)[1:]
        bottom = get(slots[1, dx], 0, 16).astype(F32).reshape(2, 8, C)[:1]
        return jnp.concatenate([top, middle, bottom], axis=0)

    left, centre, right = column(-1), column(0), column(1)
    before = pltpu.roll(jnp.where(lane_x == 7, left, centre), 1, 1)
    after = pltpu.roll(jnp.where(lane_x == 0, right, centre), 7, 1)
    for d, rows in enumerate((before, centre, after)):
        even[d, i, z] = rows[1:9].reshape(64, C).astype(BF)
        odd[d, i, z] = rows.reshape(80, C).astype(BF)


def shifted(even, odd, tap, brick=None):
    tz, ty, tx = tap // 9, tap // 3 % 3, tap % 3
    which = slice(None) if brick is None else brick
    count = SLOTS if brick is None else 1
    if ty == 1:
        cells = even[tx, which, tz : tz + 8]
    else:
        cells = odd[tx, which, tz : tz + 8, 8 * ty : 8 * ty + 64]
    return cells.reshape(count * CELLS, C)


def encode(rows):
    index = lax.broadcasted_iota(jnp.int32, rows.shape, 1)
    top = jnp.max(jnp.where(index < CHUNK, jnp.abs(rows), 0.0), axis=1, keepdims=True)
    power = jnp.ceil(jnp.log2(jnp.maximum(top, 2.0**-100)))
    codes = jnp.round(rows * jnp.exp2(BITS - power))
    codes = jnp.where(index < CHUNK, codes, jnp.broadcast_to(power, rows.shape))
    return codes.astype(jnp.int32).astype(jnp.int16)


def decode(codes):
    values = codes.astype(jnp.int32).astype(F32)
    return values * jnp.exp2(values[:, CHUNK : CHUNK + 1] - BITS)


def main_kernel(
    coords, code, feat, cot, kernel, out, dx, gathered,
    V, U, HV, HU, HC, mine_c, near, KV, even_v, odd_v, even_u, odd_u, cot_t, edge_t, terms, grad, sibling,
    out_codes, in_codes, mid_codes, mid_in,
    load_sem, halo_send, halo_recv, core_send, core_recv, s1, r1, s2, r2, s3, r3, hand_send, hand_recv,
):
    slab = lax.axis_index("slab")
    z, x, core, y = place()
    me = (x * 8 + y, x * 8 + z)
    ring_me = (z, y)

    other = device(z, x, 1 - core, y)
    has_lower, has_upper = slab > 0, slab < 63
    lower, upper = {"slab": lax.rem(slab + 63, 64)}, {"slab": lax.rem(slab + 1, 64)}

    near_x = [(x + step) & 3 for step in range(4)]
    near_y, near_z = [(y + step) & 7 for step in range(8)], [(z + step) & 7 for step in range(8)]

    def team(kind):
        for step_x in range(4):
            for step in range(8):
                if step_x or step:
                    row, column = near_x[step_x], (near_y, near_z)[kind][step]
                    where = device(z, row, core, column) if kind == 0 else device(column, row, core, y)
                    yield row * 8 + column, where

    def ring(kind):
        for step in range(1, 8):
            yield device(near_z[step], x, core, y) if kind == 0 else device(z, x, core, near_y[step])

    barrier = pltpu.get_barrier_semaphore()
    pl.semaphore_signal(barrier, inc=1, device_id=other, device_id_type=MESH)

    @pl.when(has_upper & (core == 1))
    def _():
        pl.semaphore_signal(barrier, inc=1, device_id=upper, device_id_type=MESH)

    @pl.when(has_lower & (core == 0))
    def _():
        pl.semaphore_signal(barrier, inc=1, device_id=lower, device_id_type=MESH)

    for kind in range(2):
        for _, peer in team(kind):
            pl.semaphore_signal(barrier, inc=1, device_id=peer, device_id_type=MESH)

    loads = [
        pltpu.make_async_copy(feat, V.at[pl.ds(0, SLOTS)], load_sem.at[0]),
        pltpu.make_async_copy(cot, U.at[pl.ds(0, SLOTS)], load_sem.at[1]),
        pltpu.make_async_copy(kernel, KV, load_sem.at[2]),
    ]
    for load in loads:
        load.start()
    for cells in (V, U):
        cells[SLOTS] = jnp.zeros((8, 64, C), BF)
    for planes in (HV, HU):
        for d in range(2):
            planes[d, SLOTS] = jnp.zeros((64, C), BF)
    for z0 in (0, 9):
        even_v[:, :, z0] = jnp.zeros((3, SLOTS, 64, C), BF)
        odd_v[:, :, z0] = jnp.zeros((3, SLOTS, 80, C), BF)
    lane = lax.broadcasted_iota(jnp.int32, (8, C), 1)
    row = jnp.full((8, C), 16, jnp.int32)
    for k in range(SLOTS):
        row = jnp.where(lane == k, coords[0, k], row)
    mine_c[...] = row
    flip_code = code[0]
    flip_x, flip_y, flip_z = flip_code & 1, (flip_code >> 1) & 1, (flip_code >> 2) & 1

    def mirrored(tap):
        tz, ty, tx = tap // 9, tap // 3 % 3, tap % 3
        return tap + flip_z * (18 - 18 * tz) + flip_y * (6 - 6 * ty) + flip_x * (2 - 2 * tx)

    def inner(cells, even, odd):
        @pl.loop(0, SLOTS)
        def _(i):
            slots = neighbours(lambda k: coords[0, k], coords[0, i])

            @pl.loop(0, 8)
            def _(plane):
                build_plane(lambda j, a, n: cells[j, plane, pl.ds(a, n), :], slots, even, odd, i, plane + 1)

    def outer(planes, even, odd):
        @pl.loop(0, SLOTS)
        def _(i):
            for d, plane, there in ((0, 0, has_lower), (1, 9, has_upper)):
                slots = neighbours(lambda k: jnp.where(there, near[d, 0, k], 16), coords[0, i])
                build_plane(lambda j, a, n: planes[d, j, pl.ds(a, n), :], slots, even, odd, i, plane)

    loads[0].wait()
    inner(V, even_v, odd_v)
    loads[1].wait()
    zero = jnp.zeros((), BF)
    for i in range(SLOTS):
        cells = jnp.where(coords[0, i] < 16, U[i].reshape(CELLS, C), zero)
        cot_t[:, i * CELLS : (i + 1) * CELLS] = cells.T
    for d, plane in ((0, 0), (1, 7)):
        edge = [jnp.where(coords[0, i] < 16, U[i, plane], zero) for i in range(SLOTS)]
        edge_t[d] = jnp.concatenate(edge, axis=0).T
    def products(taps, left, read):
        for first in range(0, len(taps), 2):
            two = taps[first : first + 2]
            cols = jnp.concatenate([read(t) for t in two], axis=1)
            sums = jnp.dot(left, cols, preferred_element_type=F32)
            for k, t in enumerate(two):
                yield t, sums[:, k * C : (k + 1) * C].T

    def fill(part):
        for n, t in enumerate(ORDER[part]):
            grad[part, n * C : (n + 1) * C] = terms[mirrored(t)]

    for t, term in products(MIDDLE + LOW + HIGH, cot_t[...], lambda t: shifted(even_v, odd_v, t)):
        terms[t] = term
    fill(0)
    for n in range(len(ORDER[PARTS - 1]), PART_TAPS):
        grad[PARTS - 1, n * C : (n + 1) * C] = jnp.zeros((C, C), F32)

    half = PART_TAPS * C // 2

    def to_core(part):
        src = grad.at[part, pl.ds(pl.multiple_of((1 - core) * half, 8), half)]
        return remote(src, sibling.at[part, pl.ds(0, half)], core_send.at[part], core_recv.at[part], other)

    inner(U, even_u, odd_u)
    pl.semaphore_wait(barrier, 2 * GROUP - 1 + ((has_upper & (core == 1)) | (has_lower & (core == 0))).astype(jnp.int32))

    halos = []
    for d, (there, peer, plane) in enumerate(((has_upper, upper, 7), (has_lower, lower, 0))):
        group = [
            remote(mine_c, HC.at[d], halo_send.at[d, 0], halo_recv.at[d, 0], peer),
            remote(feat.at[:, plane], HV.at[d, pl.ds(0, SLOTS)], halo_send.at[d, 1], halo_recv.at[d, 1], peer),
            remote(cot.at[:, plane], HU.at[d, pl.ds(0, SLOTS)], halo_send.at[d, 2], halo_recv.at[d, 2], peer),
        ]
        halos.append((there, group))

    def start_halo(k):
        for there, group in halos:
            pl.when(there)(group[k].start)

    def end_halo(k):
        for (there, _), (_, group) in zip(reversed(halos), halos, strict=True):
            pl.when(there)(group[k].wait_recv)

    start_halo(0)
    start_halo(1)
    to_core(0).start()
    start_halo(2)

    def scatter(part):
        landing = in_codes.at[part, me[part % 2]]
        for j, peer in team(part % 2):
            remote(out_codes.at[part, j], landing, s1.at[part], r1.at[part], peer).start()

    def send_part(part):
        to_core(part).wait_recv()

        @pl.loop(0, GROUP // 8)
        def _(eight):
            base = pl.multiple_of(eight * 8 * CHUNK, 8)
            mine = grad[part, pl.ds(pl.multiple_of(core * half + base, 8), 120)]
            rows = mine + sibling[part, pl.ds(base, 120)]
            blocks = jnp.stack([rows[n * CHUNK : n * CHUNK + ROWS] for n in range(8)])
            out_codes[part, pl.ds(eight * 8, 8)] = encode(blocks)

        scatter(part)

    send_part(0)

    end_halo(0)
    near_copy = pltpu.make_async_copy(HC, near, load_sem.at[3])
    near_copy.start()
    end_halo(1)
    near_copy.wait()
    outer(HV, even_v, odd_v)

    def edge_cells(t):
        ty, tx, side = t // 3 % 3, t % 3, 9 * (t // 18)
        if ty == 1:
            return even_v[tx, :, side].reshape(SLOTS * 64, C)
        return odd_v[tx, :, side, 8 * ty : 8 * ty + 64].reshape(SLOTS * 64, C)

    for d, taps in enumerate((LOW, HIGH)):
        for t, term in products(taps, edge_t[d], edge_cells):
            terms[t] += term
    for part in range(1, PARTS):
        fill(part)
        to_core(part).start()
    for part in range(1, PARTS):
        send_part(part)

    def convolve(i, backward):
        total = jnp.zeros((CELLS, C), F32)
        for first in range(0, TAPS, 2):
            taps = range(first, min(first + 2, TAPS))
            if backward:
                cols = jnp.concatenate([shifted(even_u, odd_u, 26 - t, i) for t in taps], axis=1)
                weights = jnp.concatenate([KV[mirrored(t)] for t in taps], axis=1)
                dims = (((1,), (1,)), ((), ()))
            else:
                cols = jnp.concatenate([shifted(even_v, odd_v, t, i) for t in taps], axis=1)
                weights = jnp.concatenate([KV[mirrored(t)] for t in taps], axis=0)
                dims = (((1,), (0,)), ((), ()))
            total += lax.dot_general(cols, weights, dims, preferred_element_type=F32)
        return jnp.where(coords[0, i] < 16, total, 0.0).astype(BF).reshape(8, 64, C)

    loads[2].wait()

    @pl.loop(0, SLOTS)
    def _(i):
        out[i] = convolve(i, False)

    end_halo(2)
    outer(HU, even_u, odd_u)

    def exchange(part):
        landing = mid_in.at[part, ring_me[part % 2]]
        for peer in ring(part % 2):
            remote(mid_codes.at[part], landing, s2.at[part], r2.at[part], peer).start()

    def several(buffer, count, send, recv):
        blocks = buffer.at[pl.ds(0, count)]
        return remote(blocks, blocks, send, recv, other)

    for part in range(PARTS):
        kind = part % 2
        several(in_codes.at[part], GROUP - 1, s1.at[part], r1.at[part]).wait_recv()

        in_codes[part, me[kind]] = out_codes[part, me[kind]]

        def add(eight, total):
            return total + jnp.sum(decode(in_codes[part, pl.ds(eight * 8, 8)]), axis=0, keepdims=True)

        total = lax.fori_loop(0, GROUP // 8, add, jnp.zeros((1, ROWS, C), F32))
        codes = encode(total)[0]
        mid_codes[part] = codes
        mid_in[part, ring_me[kind]] = codes

        exchange(part)

    @pl.loop(0, 2)
    def _(i):
        dx[i] = convolve(i, True)

    def publish(part):
        block = gathered.at[part, core, me[part % 2]]
        for _, peer in team(part % 2):
            remote(block, block, s3.at[part], r3.at[part], peer).start()

    for part in range(PARTS):
        kind = part % 2
        several(mid_in.at[part], 7, s2.at[part], r2.at[part]).wait_recv()
        total = jnp.sum(decode(mid_in[part]), axis=0, keepdims=True)
        gathered[part, core, me[kind]] = encode(total)[0]

        publish(part)

    @pl.loop(2, SLOTS)
    def _(i):
        dx[i] = convolve(i, True)

    def hand(part):
        block = gathered.at[part, core]
        return remote(block, block, hand_send.at[part], hand_recv.at[part], other)

    for part in range(PARTS):
        several(gathered.at[part, core], GROUP - 1, s3.at[part], r3.at[part]).wait_recv()
        hand(part).start()

    for part in range(PARTS):
        to_core(part).wait_send()
        several(out_codes.at[part], GROUP - 1, s1.at[part], r1.at[part]).wait_send()
        several(mid_in.at[part], 7, s2.at[part], r2.at[part]).wait_send()
        several(gathered.at[part, core], GROUP - 1, s3.at[part], r3.at[part]).wait_send()
        hand(part).wait_send()
    for there, group in halos:
        for copy in group:
            pl.when(there)(copy.wait_send)
    for part in range(PARTS):
        hand(part).wait_recv()


def main_call(coords, code, feat, cot, kernel):
    smem, vmem = pl.BlockSpec(memory_space=pltpu.SMEM), pl.BlockSpec(memory_space=pltpu.VMEM)
    anywhere = pl.BlockSpec(memory_space=pl.ANY)
    dma = pltpu.SemaphoreType.DMA
    cells, planes = pltpu.VMEM((SLOTS + 1, 8, 64, C), BF), pltpu.VMEM((2, SLOTS + 1, 64, C), BF)
    even, odd = pltpu.VMEM((3, SLOTS, 10, 64, C), BF), pltpu.VMEM((3, SLOTS, 10, 80, C), BF)
    codes = pltpu.VMEM((PARTS, GROUP, ROWS, C), jnp.int16)
    return pl.pallas_call(
        main_kernel,
        out_shape=[
            pltpu.VMEM((SLOTS, 8, 64, C), BF),
            pltpu.VMEM((SLOTS, 8, 64, C), BF),
            pltpu.VMEM((PARTS, 2, GROUP, ROWS, C), jnp.int16),
        ],
        in_specs=[smem] * 2 + [anywhere] * 3,
        out_specs=[vmem] * 3,
        scratch_shapes=[
            cells, cells, planes, planes, pltpu.VMEM((2, 8, C), jnp.int32), pltpu.VMEM((8, C), jnp.int32),
            pltpu.SMEM((2, 8, C), jnp.int32), pltpu.VMEM((TAPS, C, C), BF), even, odd, even, odd,
            pltpu.VMEM((C, SLOTS * CELLS), BF), pltpu.VMEM((2, C, SLOTS * 64), BF), pltpu.VMEM((TAPS, C, C), F32),
            pltpu.VMEM((PARTS, PART_TAPS * C + 8, C), F32), pltpu.VMEM((PARTS, PART_TAPS * C // 2 + 8, C), F32),
            codes, codes, pltpu.VMEM((PARTS, ROWS, C), jnp.int16), pltpu.VMEM((PARTS, 8, ROWS, C), jnp.int16),
            dma((4,)), dma((2, 3)), dma((2, 3)), dma((PARTS,)), dma((PARTS,)), dma((PARTS,)), dma((PARTS,)),
            dma((PARTS,)), dma((PARTS,)), dma((PARTS,)), dma((PARTS,)), dma((PARTS,)), dma((PARTS,)),
        ],
        compiler_params=pltpu.CompilerParams(collective_id=0, has_side_effects=True, vmem_limit_bytes=60 << 20),
        name="brick_convs",
    )(coords, code, feat, cot, kernel)


def result_kernel(scale, out_in, dx_in, codes, out, dx, grad, rows, sems):
    copies = [pltpu.make_async_copy(out_in, out, sems.at[0]), pltpu.make_async_copy(dx_in, dx, sems.at[1])]
    for copy in copies:
        copy.start()
    half = PART_TAPS * C // 2
    stores = []
    for part in range(PARTS):
        for core in range(2):

            @pl.loop(0, GROUP // 8)
            def _(eight):
                blocks = decode(codes[part, core, pl.ds(eight * 8, 8)]) * scale
                start = pl.multiple_of(core * half + eight * 8 * CHUNK, 8)
                rows[part, pl.ds(start, 8 * CHUNK)] = jnp.concatenate([blocks[n, :CHUNK] for n in range(8)], axis=0)

        first = 0
        taps = ORDER[part]
        for n in range(1, len(taps) + 1):
            if n == len(taps) or taps[n] != taps[n - 1] + 1:
                store = pltpu.make_async_copy(
                    rows.at[part, pl.ds(first * C, (n - first) * C)],
                    grad.at[pl.ds(taps[first] * C, (n - first) * C)],
                    sems.at[2 + len(stores)],
                )
                store.start()
                stores.append(store)
                first = n
    for copy in stores + copies:
        copy.wait()


def results(out, dx, codes, scale):
    anywhere, vmem = pl.BlockSpec(memory_space=pl.ANY), pl.BlockSpec(memory_space=pltpu.VMEM)
    return pl.pallas_call(
        functools.partial(result_kernel, scale),
        out_shape=[
            jax.ShapeDtypeStruct((SLOTS, 8, 64, C), BF),
            jax.ShapeDtypeStruct((SLOTS, 8, 64, C), BF),
            jax.ShapeDtypeStruct((TAPS * C, C), F32),
        ],
        in_specs=[vmem] * 3,
        out_specs=[anywhere] * 3,
        scratch_shapes=[
            pltpu.VMEM((PARTS, PART_TAPS * C, C), F32),
            pltpu.SemaphoreType.DMA((2 + 4 * PARTS,)),
        ],
        compiler_params=pltpu.CompilerParams(vmem_limit_bytes=48 << 20),
        name="results",
    )(out, dx, codes)


def shards(features, cotangent, coords, orientation, kernel):
    feat = features.reshape(SLOTS, 8, 64, C)
    cot = cotangent.reshape(SLOTS, 8, 64, C)
    out, dx, codes = main_call(coords, orientation, feat, cot, kernel)
    out, dx, total = results(out, dx, codes, float(8 * 64 * 2 * 512) ** -0.5)
    shape = (1, SLOTS, CELLS, C)
    return out.reshape(shape), dx.reshape(shape), total


def solution(mesh):
    in_specs = (
        P("batch", "slab", None, None),
        P("batch", "slab", None, None),
        P("batch", "slab"),
        P("batch"),
        P(),
    )
    out_specs = (P("batch", "slab", None, None), P("batch", "slab", None, None), P())
    return jax.shard_map(shards, mesh=mesh, in_specs=in_specs, out_specs=out_specs, check_vma=False)
```

```python
import functools

import jax
import jax.numpy as jnp
from jax import lax
from jax.experimental import pallas as pl
from jax.experimental.pallas import tpu as pltpu
from jax.sharding import PartitionSpec as P

C = 128
SLOTS = 4
CELLS = 512
TAPS = 27
GROUP = 32
PARTS = 4
PART_TAPS = 7
CHUNK = PART_TAPS * C // 2 // GROUP
ROWS = 16
BITS = 14.95
MIDDLE, LOW, HIGH = list(range(9, 18)), list(range(9)), list(range(18, 27))
ORDER = [list(range(9, 16)), [16, 17, 0, 1, 2, 3, 4], [5, 6, 7, 8, 18, 19, 20], list(range(21, 27))]
BF = jnp.bfloat16
F32 = jnp.float32
MESH = pl.DeviceIdType.MESH


def place():
    s = lax.axis_index("slab")
    return s // 8, (s // 2) & 3, s & 1, lax.axis_index("batch")


def device(z, x, core, y):
    return {"slab": z * 8 + x * 2 + core, "batch": y}


def remote(src, dst, send, recv, where):
    return pltpu.make_async_remote_copy(
        src_ref=src, dst_ref=dst, send_sem=send, recv_sem=recv, device_id=where, device_id_type=MESH
    )


def around(pos):
    row, col = pos >> 2, pos & 3
    inside_y = {-1: row > 0, 0: pos < 16, 1: row < 3}
    inside_x = {-1: col > 0, 0: pos < 16, 1: col < 3}
    return {
        (dy, dx): jnp.where(inside_y[dy] & inside_x[dx] & (pos < 16), pos + 4 * dy + dx, 99)
        for dy in (-1, 0, 1)
        for dx in (-1, 0, 1)
    }


def slots_of(wanted, coord):
    slots = {}
    for offset, position in wanted.items():
        slot = jnp.int32(SLOTS)
        for k in range(SLOTS):
            slot = jnp.where(coord[k] == position, k, slot)
        slots[offset] = slot
    return slots


def build_plane(get, slots, even, odd, i, z):
    lane_x = lax.broadcasted_iota(jnp.int32, (10, 8, C), 1)

    def column(dx):
        middle = get(slots[0, dx], 0, 64).astype(F32).reshape(8, 8, C)
        top = get(slots[-1, dx], 48, 16).astype(F32).reshape(2, 8, C)[1:]
        bottom = get(slots[1, dx], 0, 16).astype(F32).reshape(2, 8, C)[:1]
        return jnp.concatenate([top, middle, bottom], axis=0)

    left, centre, right = column(-1), column(0), column(1)
    before = pltpu.roll(jnp.where(lane_x == 7, left, centre), 1, 1)
    after = pltpu.roll(jnp.where(lane_x == 0, right, centre), 7, 1)
    for d, rows in enumerate((before, centre, after)):
        even[d, i, z] = rows[1:9].reshape(64, C).astype(BF)
        odd[d, i, z] = rows.reshape(80, C).astype(BF)


def shifted(even, odd, tap, brick=None):
    tz, ty, tx = tap // 9, tap // 3 % 3, tap % 3
    which = slice(None) if brick is None else brick
    count = SLOTS if brick is None else 1
    if ty == 1:
        cells = even[tx, which, tz : tz + 8]
    else:
        cells = odd[tx, which, tz : tz + 8, 8 * ty : 8 * ty + 64]
    return cells.reshape(count * CELLS, C)


def encode(rows):
    index = lax.broadcasted_iota(jnp.int32, rows.shape, 1)
    top = jnp.max(jnp.where(index < CHUNK, jnp.abs(rows), 0.0), axis=1, keepdims=True)
    power = jnp.ceil(jnp.log2(jnp.maximum(top, 2.0**-100)))
    codes = jnp.round(rows * jnp.exp2(BITS - power))
    codes = jnp.where(index < CHUNK, codes, jnp.broadcast_to(power, rows.shape))
    return codes.astype(jnp.int32).astype(jnp.int16)


def decode(codes):
    values = codes.astype(jnp.int32).astype(F32)
    return values * jnp.exp2(values[:, CHUNK : CHUNK + 1] - BITS)


def main_kernel(
    coords, code, feat, cot, kernel, out, dx, gathered,
    V, U, HV, HU, HC, mine_c, near, KV, even_v, odd_v, even_u, odd_u, cot_t, edge_t, terms, grad, sibling,
    out_codes, in_codes, mid_codes, mid_in,
    load_sem, halo_send, halo_recv, core_send, core_recv, s1, r1, s2, r2, s3, r3, hand_send, hand_recv,
):
    slab = lax.axis_index("slab")
    z, x, core, y = place()
    me = (x * 8 + y, x * 8 + z)
    ring_me = (z, y)

    other = device(z, x, 1 - core, y)
    has_lower, has_upper = slab > 0, slab < 63
    lower, upper = {"slab": lax.rem(slab + 63, 64)}, {"slab": lax.rem(slab + 1, 64)}

    near_x = [(x + step) & 3 for step in range(4)]
    near_y, near_z = [(y + step) & 7 for step in range(8)], [(z + step) & 7 for step in range(8)]

    def team(kind):
        for step in (4, 3, 5, 2, 6, 1, 7, 0):
            for step_x in (2, 1, 3, 0):
                if step_x or step:
                    row, column = near_x[step_x], (near_y, near_z)[kind][step]
                    where = device(z, row, core, column) if kind == 0 else device(column, row, core, y)
                    yield row * 8 + column, where

    def ring(kind):
        for step in range(1, 8):
            yield device(near_z[step], x, core, y) if kind == 0 else device(z, x, core, near_y[step])

    loads = [
        pltpu.make_async_copy(feat, V.at[pl.ds(0, SLOTS)], load_sem.at[0]),
        pltpu.make_async_copy(cot, U.at[pl.ds(0, SLOTS)], load_sem.at[1]),
        pltpu.make_async_copy(kernel, KV, load_sem.at[2]),
    ]
    for load in loads:
        load.start()
    barrier = pltpu.get_barrier_semaphore()
    pl.semaphore_signal(barrier, inc=1, device_id=other, device_id_type=MESH)

    @pl.when(has_upper & (core == 1))
    def _():
        pl.semaphore_signal(barrier, inc=1, device_id=upper, device_id_type=MESH)

    @pl.when(has_lower & (core == 0))
    def _():
        pl.semaphore_signal(barrier, inc=1, device_id=lower, device_id_type=MESH)

    for kind in range(2):
        for _, peer in team(kind):
            pl.semaphore_signal(barrier, inc=1, device_id=peer, device_id_type=MESH)

    for cells in (V, U):
        cells[SLOTS] = jnp.zeros((8, 64, C), BF)
    for planes in (HV, HU):
        for d in range(2):
            planes[d, SLOTS] = jnp.zeros((64, C), BF)
    for z0 in (0, 9):
        even_v[:, :, z0] = jnp.zeros((3, SLOTS, 64, C), BF)
        odd_v[:, :, z0] = jnp.zeros((3, SLOTS, 80, C), BF)
    lane = lax.broadcasted_iota(jnp.int32, (8, C), 1)
    row = jnp.full((8, C), 16, jnp.int32)
    for k in range(SLOTS):
        row = jnp.where(lane == k, coords[0, k], row)
    mine_c[...] = row
    flip_code = code[0]
    flip_x, flip_y, flip_z = flip_code & 1, (flip_code >> 1) & 1, (flip_code >> 2) & 1

    def mirrored(tap):
        tz, ty, tx = tap // 9, tap // 3 % 3, tap % 3
        return tap + flip_z * (18 - 18 * tz) + flip_y * (6 - 6 * ty) + flip_x * (2 - 2 * tx)

    def inner(cells, even, odd):
        own = [coords[0, k] for k in range(SLOTS)]

        @pl.loop(0, SLOTS)
        def _(i):
            slots = slots_of(around(coords[0, i]), own)

            @pl.loop(0, 8)
            def _(plane):
                build_plane(lambda j, a, n: cells[j, plane, pl.ds(a, n), :], slots, even, odd, i, plane + 1)

    def outer(planes, even, odd):
        sides = [[jnp.where(there, near[d, 0, k], 16) for k in range(SLOTS)] for d, there in ((0, has_lower), (1, has_upper))]

        @pl.loop(0, SLOTS)
        def _(i):
            wanted = around(coords[0, i])
            for d, plane in ((0, 0), (1, 9)):
                slots = slots_of(wanted, sides[d])
                build_plane(lambda j, a, n: planes[d, j, pl.ds(a, n), :], slots, even, odd, i, plane)

    loads[0].wait()
    inner(V, even_v, odd_v)
    loads[1].wait()
    zero = jnp.zeros((), BF)
    for i in range(SLOTS):
        cells = jnp.where(coords[0, i] < 16, U[i].reshape(CELLS, C), zero)
        cot_t[:, i * CELLS : (i + 1) * CELLS] = cells.T
    for d, plane in ((0, 0), (1, 7)):
        edge = [jnp.where(coords[0, i] < 16, U[i, plane], zero) for i in range(SLOTS)]
        edge_t[d] = jnp.concatenate(edge, axis=0).T
    def products(taps, left, read):
        for first in range(0, len(taps), 2):
            two = taps[first : first + 2]
            cols = jnp.concatenate([read(t) for t in two], axis=1)
            sums = jnp.dot(left, cols, preferred_element_type=F32)
            for k, t in enumerate(two):
                yield t, sums[:, k * C : (k + 1) * C].T

    def fill(part):
        for n, t in enumerate(ORDER[part]):
            grad[part, n * C : (n + 1) * C] = terms[mirrored(t)]

    def own_terms(taps):
        for t, term in products(taps, cot_t[...], lambda t: shifted(even_v, odd_v, t)):
            terms[t] = term

    own_terms(MIDDLE)
    fill(0)

    half = PART_TAPS * C // 2

    def to_core(part):
        src = grad.at[part, pl.ds(pl.multiple_of((1 - core) * half, 8), half)]
        return remote(src, sibling.at[part, pl.ds(0, half)], core_send.at[part], core_recv.at[part], other)

    pl.semaphore_wait(barrier, 2 * GROUP - 1 + ((has_upper & (core == 1)) | (has_lower & (core == 0))).astype(jnp.int32))

    halos = []
    for d, (there, peer, plane) in enumerate(((has_upper, upper, 7), (has_lower, lower, 0))):
        group = [
            remote(mine_c, HC.at[d], halo_send.at[d, 0], halo_recv.at[d, 0], peer),
            remote(feat.at[:, plane], HV.at[d, pl.ds(0, SLOTS)], halo_send.at[d, 1], halo_recv.at[d, 1], peer),
            remote(cot.at[:, plane], HU.at[d, pl.ds(0, SLOTS)], halo_send.at[d, 2], halo_recv.at[d, 2], peer),
        ]
        halos.append((there, group))

    def start_halo(k):
        for there, group in halos:
            pl.when(there)(group[k].start)

    def end_halo(k):
        for (there, _), (_, group) in zip(reversed(halos), halos, strict=True):
            pl.when(there)(group[k].wait_recv)

    start_halo(0)
    start_halo(1)
    to_core(0).start()
    start_halo(2)

    def scatter(part):
        landing = in_codes.at[part, me[part % 2]]
        for j, peer in team(part % 2):
            remote(out_codes.at[part, j], landing, s1.at[part], r1.at[part], peer).start()

    def send_part(part):
        to_core(part).wait_recv()

        @pl.loop(0, GROUP // 8)
        def _(eight):
            base = pl.multiple_of(eight * 8 * CHUNK, 8)
            mine = grad[part, pl.ds(pl.multiple_of(core * half + base, 8), 120)]
            rows = mine + sibling[part, pl.ds(base, 120)]
            blocks = jnp.stack([rows[n * CHUNK : n * CHUNK + ROWS] for n in range(8)])
            out_codes[part, pl.ds(eight * 8, 8)] = encode(blocks)

        scatter(part)

    own_terms(LOW + HIGH)
    for n in range(len(ORDER[PARTS - 1]), PART_TAPS):
        grad[PARTS - 1, n * C : (n + 1) * C] = jnp.zeros((C, C), F32)
    send_part(0)
    inner(U, even_u, odd_u)

    end_halo(0)
    near_copy = pltpu.make_async_copy(HC, near, load_sem.at[3])
    near_copy.start()
    end_halo(1)
    near_copy.wait()
    outer(HV, even_v, odd_v)

    def edge_cells(t):
        ty, tx, side = t // 3 % 3, t % 3, 9 * (t // 18)
        if ty == 1:
            return even_v[tx, :, side].reshape(SLOTS * 64, C)
        return odd_v[tx, :, side, 8 * ty : 8 * ty + 64].reshape(SLOTS * 64, C)

    for d, taps in enumerate((LOW, HIGH)):
        for t, term in products(taps, edge_t[d], edge_cells):
            terms[t] += term
    for part in range(1, PARTS):
        fill(part)
        to_core(part).start()
    for part in range(1, PARTS):
        send_part(part)

    def convolve(i, backward):
        total = jnp.zeros((CELLS, C), F32)
        for first in range(0, TAPS, 2):
            taps = range(first, min(first + 2, TAPS))
            if backward:
                cols = jnp.concatenate([shifted(even_u, odd_u, 26 - t, i) for t in taps], axis=1)
                weights = jnp.concatenate([KV[mirrored(t)] for t in taps], axis=1)
                dims = (((1,), (1,)), ((), ()))
            else:
                cols = jnp.concatenate([shifted(even_v, odd_v, t, i) for t in taps], axis=1)
                weights = jnp.concatenate([KV[mirrored(t)] for t in taps], axis=0)
                dims = (((1,), (0,)), ((), ()))
            total += lax.dot_general(cols, weights, dims, preferred_element_type=F32)
        return jnp.where(coords[0, i] < 16, total, 0.0).astype(BF).reshape(8, 64, C)

    loads[2].wait()

    @pl.loop(0, SLOTS)
    def _(i):
        out[i] = convolve(i, False)

    end_halo(2)
    outer(HU, even_u, odd_u)

    def exchange(part):
        landing = mid_in.at[part, ring_me[part % 2]]
        for peer in ring(part % 2):
            remote(mid_codes.at[part], landing, s2.at[part], r2.at[part], peer).start()

    def several(buffer, count, send, recv):
        blocks = buffer.at[pl.ds(0, count)]
        return remote(blocks, blocks, send, recv, other)

    for part in range(PARTS):
        kind = part % 2
        several(in_codes.at[part], GROUP - 1, s1.at[part], r1.at[part]).wait_recv()

        in_codes[part, me[kind]] = out_codes[part, me[kind]]

        def add(eight, total):
            return total + jnp.sum(decode(in_codes[part, pl.ds(eight * 8, 8)]), axis=0, keepdims=True)

        total = lax.fori_loop(0, GROUP // 8, add, jnp.zeros((1, ROWS, C), F32))
        codes = encode(total)[0]
        mid_codes[part] = codes
        mid_in[part, ring_me[kind]] = codes

        exchange(part)

    @pl.loop(0, 1)
    def _(i):
        dx[i] = convolve(i, True)

    def publish(part):
        block = gathered.at[part, core, me[part % 2]]
        for _, peer in team(part % 2):
            remote(block, block, s3.at[part], r3.at[part], peer).start()

    for part in range(PARTS):
        kind = part % 2
        several(mid_in.at[part], 7, s2.at[part], r2.at[part]).wait_recv()
        total = jnp.sum(decode(mid_in[part]), axis=0, keepdims=True)
        gathered[part, core, me[kind]] = encode(total)[0]

        publish(part)

    @pl.loop(1, SLOTS)
    def _(i):
        dx[i] = convolve(i, True)

    def hand(part):
        block = gathered.at[part, core]
        return remote(block, block, hand_send.at[part], hand_recv.at[part], other)

    for part in range(PARTS):
        several(gathered.at[part, core], GROUP - 1, s3.at[part], r3.at[part]).wait_recv()
        hand(part).start()

    for part in range(PARTS):
        to_core(part).wait_send()
        several(out_codes.at[part], GROUP - 1, s1.at[part], r1.at[part]).wait_send()
        several(mid_in.at[part], 7, s2.at[part], r2.at[part]).wait_send()
        several(gathered.at[part, core], GROUP - 1, s3.at[part], r3.at[part]).wait_send()
        hand(part).wait_send()
    for there, group in halos:
        for copy in group:
            pl.when(there)(copy.wait_send)
    for part in range(PARTS):
        hand(part).wait_recv()


def main_call(coords, code, feat, cot, kernel):
    smem, vmem = pl.BlockSpec(memory_space=pltpu.SMEM), pl.BlockSpec(memory_space=pltpu.VMEM)
    anywhere = pl.BlockSpec(memory_space=pl.ANY)
    dma = pltpu.SemaphoreType.DMA
    cells, planes = pltpu.VMEM((SLOTS + 1, 8, 64, C), BF), pltpu.VMEM((2, SLOTS + 1, 64, C), BF)
    even, odd = pltpu.VMEM((3, SLOTS, 10, 64, C), BF), pltpu.VMEM((3, SLOTS, 10, 80, C), BF)
    codes = pltpu.VMEM((PARTS, GROUP, ROWS, C), jnp.int16)
    return pl.pallas_call(
        main_kernel,
        out_shape=[
            pltpu.VMEM((SLOTS, 8, 64, C), BF),
            pltpu.VMEM((SLOTS, 8, 64, C), BF),
            pltpu.VMEM((PARTS, 2, GROUP, ROWS, C), jnp.int16),
        ],
        in_specs=[smem] * 2 + [anywhere] * 3,
        out_specs=[vmem] * 3,
        scratch_shapes=[
            cells, cells, planes, planes, pltpu.VMEM((2, 8, C), jnp.int32), pltpu.VMEM((8, C), jnp.int32),
            pltpu.SMEM((2, 8, C), jnp.int32), pltpu.VMEM((TAPS, C, C), BF), even, odd, even, odd,
            pltpu.VMEM((C, SLOTS * CELLS), BF), pltpu.VMEM((2, C, SLOTS * 64), BF), pltpu.VMEM((TAPS, C, C), F32),
            pltpu.VMEM((PARTS, PART_TAPS * C + 8, C), F32), pltpu.VMEM((PARTS, PART_TAPS * C // 2 + 8, C), F32),
            codes, codes, pltpu.VMEM((PARTS, ROWS, C), jnp.int16), pltpu.VMEM((PARTS, 8, ROWS, C), jnp.int16),
            dma((4,)), dma((2, 3)), dma((2, 3)), dma((PARTS,)), dma((PARTS,)), dma((PARTS,)), dma((PARTS,)),
            dma((PARTS,)), dma((PARTS,)), dma((PARTS,)), dma((PARTS,)), dma((PARTS,)), dma((PARTS,)),
        ],
        compiler_params=pltpu.CompilerParams(collective_id=0, has_side_effects=True, vmem_limit_bytes=60 << 20),
        name="brick_convs",
    )(coords, code, feat, cot, kernel)


def result_kernel(scale, out_in, dx_in, codes, out, dx, grad, rows, sems):
    copies = [pltpu.make_async_copy(out_in, out, sems.at[0]), pltpu.make_async_copy(dx_in, dx, sems.at[1])]
    for copy in copies:
        copy.start()
    half = PART_TAPS * C // 2
    stores = []
    for part in range(PARTS):
        for core in range(2):

            @pl.loop(0, GROUP // 8)
            def _(eight):
                blocks = decode(codes[part, core, pl.ds(eight * 8, 8)]) * scale
                start = pl.multiple_of(core * half + eight * 8 * CHUNK, 8)
                rows[part, pl.ds(start, 8 * CHUNK)] = jnp.concatenate([blocks[n, :CHUNK] for n in range(8)], axis=0)

        first = 0
        taps = ORDER[part]
        for n in range(1, len(taps) + 1):
            if n == len(taps) or taps[n] != taps[n - 1] + 1:
                store = pltpu.make_async_copy(
                    rows.at[part, pl.ds(first * C, (n - first) * C)],
                    grad.at[pl.ds(taps[first] * C, (n - first) * C)],
                    sems.at[2 + len(stores)],
                )
                store.start()
                stores.append(store)
                first = n
    for copy in stores + copies:
        copy.wait()


def results(out, dx, codes, scale):
    anywhere, vmem = pl.BlockSpec(memory_space=pl.ANY), pl.BlockSpec(memory_space=pltpu.VMEM)
    return pl.pallas_call(
        functools.partial(result_kernel, scale),
        out_shape=[
            jax.ShapeDtypeStruct((SLOTS, 8, 64, C), BF),
            jax.ShapeDtypeStruct((SLOTS, 8, 64, C), BF),
            jax.ShapeDtypeStruct((TAPS * C, C), F32),
        ],
        in_specs=[vmem] * 3,
        out_specs=[anywhere] * 3,
        scratch_shapes=[
            pltpu.VMEM((PARTS, PART_TAPS * C, C), F32),
            pltpu.SemaphoreType.DMA((2 + 4 * PARTS,)),
        ],
        compiler_params=pltpu.CompilerParams(vmem_limit_bytes=48 << 20),
        name="results",
    )(out, dx, codes)


def shards(features, cotangent, coords, orientation, kernel):
    feat = features.reshape(SLOTS, 8, 64, C)
    cot = cotangent.reshape(SLOTS, 8, 64, C)
    out, dx, codes = main_call(coords, orientation, feat, cot, kernel)
    out, dx, total = results(out, dx, codes, float(8 * 64 * 2 * 512) ** -0.5)
    shape = (1, SLOTS, CELLS, C)
    return out.reshape(shape), dx.reshape(shape), total


def solution(mesh):
    in_specs = (
        P("batch", "slab", None, None),
        P("batch", "slab", None, None),
        P("batch", "slab"),
        P("batch"),
        P(),
    )
    out_specs = (P("batch", "slab", None, None), P("batch", "slab", None, None), P())
    return jax.shard_map(shards, mesh=mesh, in_specs=in_specs, out_specs=out_specs, check_vma=False)
```

```python
import functools

import jax
import jax.numpy as jnp
from jax import lax
from jax.experimental import pallas as pl
from jax.experimental.pallas import tpu as pltpu
from jax.sharding import PartitionSpec as P

C = 128
SLOTS = 4
CELLS = 512
TAPS = 27
GROUP = 32
PARTS = 4
PART_TAPS = 7
CHUNK = PART_TAPS * C // 2 // GROUP
ROWS = 16
BITS = 14.95
MIDDLE, LOW, HIGH = list(range(9, 18)), list(range(9)), list(range(18, 27))
ORDER = [list(range(9, 16)), [16, 17, 0, 1, 2, 3, 4], [5, 6, 7, 8, 18, 19, 20], list(range(21, 27))]
BF = jnp.bfloat16
F32 = jnp.float32
MESH = pl.DeviceIdType.MESH


def place():
    s = lax.axis_index("slab")
    return s // 8, (s // 2) & 3, s & 1, lax.axis_index("batch")


def device(z, x, core, y):
    return {"slab": z * 8 + x * 2 + core, "batch": y}


def remote(src, dst, send, recv, where):
    return pltpu.make_async_remote_copy(
        src_ref=src, dst_ref=dst, send_sem=send, recv_sem=recv, device_id=where, device_id_type=MESH
    )


def around(pos):
    row, col = pos >> 2, pos & 3
    inside_y = {-1: row > 0, 0: pos < 16, 1: row < 3}
    inside_x = {-1: col > 0, 0: pos < 16, 1: col < 3}
    return {
        (dy, dx): jnp.where(inside_y[dy] & inside_x[dx] & (pos < 16), pos + 4 * dy + dx, 99)
        for dy in (-1, 0, 1)
        for dx in (-1, 0, 1)
    }


def slots_of(wanted, coord):
    slots = {}
    for offset, position in wanted.items():
        slot = jnp.int32(SLOTS)
        for k in range(SLOTS):
            slot = jnp.where(coord[k] == position, k, slot)
        slots[offset] = slot
    return slots


def build_plane(get, slots, even, odd, i, z):
    lane_x = lax.broadcasted_iota(jnp.int32, (10, 8, C), 1)

    def column(dx):
        middle = get(slots[0, dx], 0, 64).astype(F32).reshape(8, 8, C)
        top = get(slots[-1, dx], 48, 16).astype(F32).reshape(2, 8, C)[1:]
        bottom = get(slots[1, dx], 0, 16).astype(F32).reshape(2, 8, C)[:1]
        return jnp.concatenate([top, middle, bottom], axis=0)

    left, centre, right = column(-1), column(0), column(1)
    before = pltpu.roll(jnp.where(lane_x == 7, left, centre), 1, 1)
    after = pltpu.roll(jnp.where(lane_x == 0, right, centre), 7, 1)
    for d, rows in enumerate((before, centre, after)):
        even[d, i, z] = rows[1:9].reshape(64, C).astype(BF)
        odd[d, i, z] = rows.reshape(80, C).astype(BF)


def shifted(even, odd, tap, brick=None):
    tz, ty, tx = tap // 9, tap // 3 % 3, tap % 3
    which = slice(None) if brick is None else brick
    count = SLOTS if brick is None else 1
    if ty == 1:
        cells = even[tx, which, tz : tz + 8]
    else:
        cells = odd[tx, which, tz : tz + 8, 8 * ty : 8 * ty + 64]
    return cells.reshape(count * CELLS, C)


def encode(rows):
    index = lax.broadcasted_iota(jnp.int32, rows.shape, 1)
    top = jnp.max(jnp.where(index < CHUNK, jnp.abs(rows), 0.0), axis=1, keepdims=True)
    power = jnp.ceil(jnp.log2(jnp.maximum(top, 2.0**-100)))
    codes = jnp.round(rows * jnp.exp2(BITS - power))
    codes = jnp.where(index < CHUNK, codes, jnp.broadcast_to(power, rows.shape))
    return codes.astype(jnp.int32).astype(jnp.int16)


def decode(codes):
    values = codes.astype(jnp.int32).astype(F32)
    return values * jnp.exp2(values[:, CHUNK : CHUNK + 1] - BITS)


def main_kernel(
    coords_in, code_in, feat, cot, kernel, out, dx, gathered,
    coords, code, V, U, HV, HU, HC, mine_c, near, KV, even_v, odd_v, even_u, odd_u, cot_t, edge_t, terms, grad, sibling,
    out_codes, in_codes, mid_codes, mid_in,
    load_sem, halo_send, halo_recv, core_send, core_recv, s1, r1, s2, r2, s3, r3, hand_send, hand_recv,
):
    slab = lax.axis_index("slab")
    z, x, core, y = place()
    me = (x * 8 + y, x * 8 + z)
    ring_me = (z, y)

    other = device(z, x, 1 - core, y)
    has_lower, has_upper = slab > 0, slab < 63
    lower, upper = {"slab": lax.rem(slab + 63, 64)}, {"slab": lax.rem(slab + 1, 64)}

    near_x = [(x + step) & 3 for step in range(4)]
    near_y, near_z = [(y + step) & 7 for step in range(8)], [(z + step) & 7 for step in range(8)]

    def team(kind):
        for step in (4, 3, 5, 2, 6, 1, 7, 0):
            for step_x in (2, 1, 3, 0):
                if step_x or step:
                    row, column = near_x[step_x], (near_y, near_z)[kind][step]
                    where = device(z, row, core, column) if kind == 0 else device(column, row, core, y)
                    yield row * 8 + column, where

    def ring(kind):
        for step in range(1, 8):
            yield device(near_z[step], x, core, y) if kind == 0 else device(z, x, core, near_y[step])

    loads = [
        pltpu.make_async_copy(feat, V.at[pl.ds(0, SLOTS)], load_sem.at[0]),
        pltpu.make_async_copy(cot, U.at[pl.ds(0, SLOTS)], load_sem.at[1]),
        pltpu.make_async_copy(kernel, KV, load_sem.at[2]),
    ]
    codes = [pltpu.make_async_copy(coords_in, coords, load_sem.at[4]), pltpu.make_async_copy(code_in, code, load_sem.at[5])]
    for load in codes + loads:
        load.start()
    barrier = pltpu.get_barrier_semaphore()
    pl.semaphore_signal(barrier, inc=1, device_id=other, device_id_type=MESH)

    @pl.when(has_upper & (core == 1))
    def _():
        pl.semaphore_signal(barrier, inc=1, device_id=upper, device_id_type=MESH)

    @pl.when(has_lower & (core == 0))
    def _():
        pl.semaphore_signal(barrier, inc=1, device_id=lower, device_id_type=MESH)

    for kind in range(2):
        for _, peer in team(kind):
            pl.semaphore_signal(barrier, inc=1, device_id=peer, device_id_type=MESH)

    for cells in (V, U):
        cells[SLOTS] = jnp.zeros((8, 64, C), BF)
    for planes in (HV, HU):
        for d in range(2):
            planes[d, SLOTS] = jnp.zeros((64, C), BF)
    for z0 in (0, 9):
        even_v[:, :, z0] = jnp.zeros((3, SLOTS, 64, C), BF)
        odd_v[:, :, z0] = jnp.zeros((3, SLOTS, 80, C), BF)
    for copy in codes:
        copy.wait()
    lane = lax.broadcasted_iota(jnp.int32, (8, C), 1)
    row = jnp.full((8, C), 16, jnp.int32)
    for k in range(SLOTS):
        row = jnp.where(lane == k, coords[0, k], row)
    mine_c[...] = row
    flip_code = code[0]
    flip_x, flip_y, flip_z = flip_code & 1, (flip_code >> 1) & 1, (flip_code >> 2) & 1

    def mirrored(tap):
        tz, ty, tx = tap // 9, tap // 3 % 3, tap % 3
        return tap + flip_z * (18 - 18 * tz) + flip_y * (6 - 6 * ty) + flip_x * (2 - 2 * tx)

    def inner(cells, even, odd):
        own = [coords[0, k] for k in range(SLOTS)]

        @pl.loop(0, SLOTS)
        def _(i):
            slots = slots_of(around(coords[0, i]), own)

            @pl.loop(0, 8)
            def _(plane):
                build_plane(lambda j, a, n: cells[j, plane, pl.ds(a, n), :], slots, even, odd, i, plane + 1)

    def outer(planes, even, odd):
        sides = [[jnp.where(there, near[d, 0, k], 16) for k in range(SLOTS)] for d, there in ((0, has_lower), (1, has_upper))]

        @pl.loop(0, SLOTS)
        def _(i):
            wanted = around(coords[0, i])
            for d, plane in ((0, 0), (1, 9)):
                slots = slots_of(wanted, sides[d])
                build_plane(lambda j, a, n: planes[d, j, pl.ds(a, n), :], slots, even, odd, i, plane)

    loads[0].wait()
    inner(V, even_v, odd_v)
    loads[1].wait()
    zero = jnp.zeros((), BF)
    for i in range(SLOTS):
        cells = jnp.where(coords[0, i] < 16, U[i].reshape(CELLS, C), zero)
        cot_t[:, i * CELLS : (i + 1) * CELLS] = cells.T
    for d, plane in ((0, 0), (1, 7)):
        edge = [jnp.where(coords[0, i] < 16, U[i, plane], zero) for i in range(SLOTS)]
        edge_t[d] = jnp.concatenate(edge, axis=0).T
    def products(taps, left, read):
        for first in range(0, len(taps), 2):
            two = taps[first : first + 2]
            cols = jnp.concatenate([read(t) for t in two], axis=1)
            sums = jnp.dot(left, cols, preferred_element_type=F32)
            for k, t in enumerate(two):
                yield t, sums[:, k * C : (k + 1) * C].T

    def fill(part):
        for n, t in enumerate(ORDER[part]):
            grad[part, n * C : (n + 1) * C] = terms[mirrored(t)]

    def own_terms(taps):
        for t, term in products(taps, cot_t[...], lambda t: shifted(even_v, odd_v, t)):
            terms[t] = term

    own_terms(MIDDLE)
    fill(0)

    half = PART_TAPS * C // 2

    def to_core(part):
        src = grad.at[part, pl.ds(pl.multiple_of((1 - core) * half, 8), half)]
        return remote(src, sibling.at[part, pl.ds(0, half)], core_send.at[part], core_recv.at[part], other)

    pl.semaphore_wait(barrier, 2 * GROUP - 1 + ((has_upper & (core == 1)) | (has_lower & (core == 0))).astype(jnp.int32))

    halos = []
    for d, (there, peer, plane) in enumerate(((has_upper, upper, 7), (has_lower, lower, 0))):
        group = [
            remote(mine_c, HC.at[d], halo_send.at[d, 0], halo_recv.at[d, 0], peer),
            remote(V.at[pl.ds(0, SLOTS), plane], HV.at[d, pl.ds(0, SLOTS)], halo_send.at[d, 1], halo_recv.at[d, 1], peer),
            remote(U.at[pl.ds(0, SLOTS), plane], HU.at[d, pl.ds(0, SLOTS)], halo_send.at[d, 2], halo_recv.at[d, 2], peer),
        ]
        halos.append((there, group))

    def start_halo(k):
        for there, group in halos:
            pl.when(there)(group[k].start)

    def end_halo(k):
        for (there, _), (_, group) in zip(reversed(halos), halos, strict=True):
            pl.when(there)(group[k].wait_recv)

    start_halo(0)
    start_halo(1)
    to_core(0).start()
    start_halo(2)

    def scatter(part):
        landing = in_codes.at[part, me[part % 2]]
        for j, peer in team(part % 2):
            remote(out_codes.at[part, j], landing, s1.at[part], r1.at[part], peer).start()

    def send_part(part):
        to_core(part).wait_recv()

        @pl.loop(0, GROUP // 8)
        def _(eight):
            base = pl.multiple_of(eight * 8 * CHUNK, 8)
            mine = grad[part, pl.ds(pl.multiple_of(core * half + base, 8), 120)]
            rows = mine + sibling[part, pl.ds(base, 120)]
            blocks = jnp.stack([rows[n * CHUNK : n * CHUNK + ROWS] for n in range(8)])
            out_codes[part, pl.ds(eight * 8, 8)] = encode(blocks)

        scatter(part)

    own_terms(LOW + HIGH)
    for n in range(len(ORDER[PARTS - 1]), PART_TAPS):
        grad[PARTS - 1, n * C : (n + 1) * C] = jnp.zeros((C, C), F32)
    send_part(0)
    inner(U, even_u, odd_u)

    end_halo(0)
    near_copy = pltpu.make_async_copy(HC, near, load_sem.at[3])
    near_copy.start()
    end_halo(1)
    near_copy.wait()
    outer(HV, even_v, odd_v)

    def edge_cells(t):
        ty, tx, side = t // 3 % 3, t % 3, 9 * (t // 18)
        if ty == 1:
            return even_v[tx, :, side].reshape(SLOTS * 64, C)
        return odd_v[tx, :, side, 8 * ty : 8 * ty + 64].reshape(SLOTS * 64, C)

    for d, taps in enumerate((LOW, HIGH)):
        for t, term in products(taps, edge_t[d], edge_cells):
            terms[t] += term
    for part in range(1, PARTS):
        fill(part)
        to_core(part).start()
    for part in range(1, PARTS):
        send_part(part)

    def convolve(i, backward):
        total = jnp.zeros((CELLS, C), F32)
        for first in range(0, TAPS, 2):
            taps = range(first, min(first + 2, TAPS))
            if backward:
                cols = jnp.concatenate([shifted(even_u, odd_u, 26 - t, i) for t in taps], axis=1)
                weights = jnp.concatenate([KV[mirrored(t)] for t in taps], axis=1)
                dims = (((1,), (1,)), ((), ()))
            else:
                cols = jnp.concatenate([shifted(even_v, odd_v, t, i) for t in taps], axis=1)
                weights = jnp.concatenate([KV[mirrored(t)] for t in taps], axis=0)
                dims = (((1,), (0,)), ((), ()))
            total += lax.dot_general(cols, weights, dims, preferred_element_type=F32)
        return jnp.where(coords[0, i] < 16, total, 0.0).astype(BF).reshape(8, 64, C)

    loads[2].wait()

    @pl.loop(0, SLOTS)
    def _(i):
        out[i] = convolve(i, False)

    end_halo(2)
    outer(HU, even_u, odd_u)

    def exchange(part):
        landing = mid_in.at[part, ring_me[part % 2]]
        for peer in ring(part % 2):
            remote(mid_codes.at[part], landing, s2.at[part], r2.at[part], peer).start()

    def several(buffer, count, send, recv):
        blocks = buffer.at[pl.ds(0, count)]
        return remote(blocks, blocks, send, recv, other)

    for part in range(PARTS):
        kind = part % 2
        several(in_codes.at[part], GROUP - 1, s1.at[part], r1.at[part]).wait_recv()

        in_codes[part, me[kind]] = out_codes[part, me[kind]]

        def add(eight, total):
            return total + jnp.sum(decode(in_codes[part, pl.ds(eight * 8, 8)]), axis=0, keepdims=True)

        total = lax.fori_loop(0, GROUP // 8, add, jnp.zeros((1, ROWS, C), F32))
        codes = encode(total)[0]
        mid_codes[part] = codes
        mid_in[part, ring_me[kind]] = codes

        exchange(part)

    @pl.loop(0, 1)
    def _(i):
        dx[i] = convolve(i, True)

    def publish(part):
        block = gathered.at[part, core, me[part % 2]]
        for _, peer in team(part % 2):
            remote(block, block, s3.at[part], r3.at[part], peer).start()

    for part in range(PARTS):
        kind = part % 2
        several(mid_in.at[part], 7, s2.at[part], r2.at[part]).wait_recv()
        total = jnp.sum(decode(mid_in[part]), axis=0, keepdims=True)
        gathered[part, core, me[kind]] = encode(total)[0]

        publish(part)

    @pl.loop(1, SLOTS)
    def _(i):
        dx[i] = convolve(i, True)

    def hand(part):
        block = gathered.at[part, core]
        return remote(block, block, hand_send.at[part], hand_recv.at[part], other)

    for part in range(PARTS):
        several(gathered.at[part, core], GROUP - 1, s3.at[part], r3.at[part]).wait_recv()
        hand(part).start()

    for part in range(PARTS):
        to_core(part).wait_send()
        several(out_codes.at[part], GROUP - 1, s1.at[part], r1.at[part]).wait_send()
        several(mid_in.at[part], 7, s2.at[part], r2.at[part]).wait_send()
        several(gathered.at[part, core], GROUP - 1, s3.at[part], r3.at[part]).wait_send()
        hand(part).wait_send()
    for there, group in halos:
        for copy in group:
            pl.when(there)(copy.wait_send)
    for part in range(PARTS):
        hand(part).wait_recv()


def main_call(coords, code, feat, cot, kernel):
    vmem = pl.BlockSpec(memory_space=pltpu.VMEM)
    anywhere = pl.BlockSpec(memory_space=pl.ANY)
    dma = pltpu.SemaphoreType.DMA
    cells, planes = pltpu.VMEM((SLOTS + 1, 8, 64, C), BF), pltpu.VMEM((2, SLOTS + 1, 64, C), BF)
    even, odd = pltpu.VMEM((3, SLOTS, 10, 64, C), BF), pltpu.VMEM((3, SLOTS, 10, 80, C), BF)
    codes = pltpu.VMEM((PARTS, GROUP, ROWS, C), jnp.int16)
    return pl.pallas_call(
        main_kernel,
        out_shape=[
            pltpu.VMEM((SLOTS, 8, 64, C), BF),
            pltpu.VMEM((SLOTS, 8, 64, C), BF),
            pltpu.VMEM((PARTS, 2, GROUP, ROWS, C), jnp.int16),
        ],
        in_specs=[anywhere] * 5,
        out_specs=[vmem] * 3,
        scratch_shapes=[
            pltpu.SMEM((1, SLOTS), jnp.int32), pltpu.SMEM((1,), jnp.int32), cells, cells, planes, planes, pltpu.VMEM((2, 8, C), jnp.int32), pltpu.VMEM((8, C), jnp.int32),
            pltpu.SMEM((2, 8, C), jnp.int32), pltpu.VMEM((TAPS, C, C), BF), even, odd, even, odd,
            pltpu.VMEM((C, SLOTS * CELLS), BF), pltpu.VMEM((2, C, SLOTS * 64), BF), pltpu.VMEM((TAPS, C, C), F32),
            pltpu.VMEM((PARTS, PART_TAPS * C + 8, C), F32), pltpu.VMEM((PARTS, PART_TAPS * C // 2 + 8, C), F32),
            codes, codes, pltpu.VMEM((PARTS, ROWS, C), jnp.int16), pltpu.VMEM((PARTS, 8, ROWS, C), jnp.int16),
            dma((6,)), dma((2, 3)), dma((2, 3)), dma((PARTS,)), dma((PARTS,)), dma((PARTS,)), dma((PARTS,)),
            dma((PARTS,)), dma((PARTS,)), dma((PARTS,)), dma((PARTS,)), dma((PARTS,)), dma((PARTS,)),
        ],
        compiler_params=pltpu.CompilerParams(collective_id=0, has_side_effects=True, vmem_limit_bytes=60 << 20),
        name="brick_convs",
    )(coords, code, feat, cot, kernel)


def result_kernel(scale, out_in, dx_in, codes, out, dx, grad, rows, sems):
    copies = [pltpu.make_async_copy(out_in, out, sems.at[0]), pltpu.make_async_copy(dx_in, dx, sems.at[1])]
    for copy in copies:
        copy.start()
    half = PART_TAPS * C // 2
    stores = []
    for part in range(PARTS):
        for core in range(2):

            @pl.loop(0, GROUP // 8)
            def _(eight):
                blocks = decode(codes[part, core, pl.ds(eight * 8, 8)]) * scale
                start = pl.multiple_of(core * half + eight * 8 * CHUNK, 8)
                rows[part, pl.ds(start, 8 * CHUNK)] = jnp.concatenate([blocks[n, :CHUNK] for n in range(8)], axis=0)

        first = 0
        taps = ORDER[part]
        for n in range(1, len(taps) + 1):
            if n == len(taps) or taps[n] != taps[n - 1] + 1:
                store = pltpu.make_async_copy(
                    rows.at[part, pl.ds(first * C, (n - first) * C)],
                    grad.at[pl.ds(taps[first] * C, (n - first) * C)],
                    sems.at[2 + len(stores)],
                )
                store.start()
                stores.append(store)
                first = n
    for copy in stores + copies:
        copy.wait()


def results(out, dx, codes, scale):
    anywhere, vmem = pl.BlockSpec(memory_space=pl.ANY), pl.BlockSpec(memory_space=pltpu.VMEM)
    return pl.pallas_call(
        functools.partial(result_kernel, scale),
        out_shape=[
            jax.ShapeDtypeStruct((SLOTS, 8, 64, C), BF),
            jax.ShapeDtypeStruct((SLOTS, 8, 64, C), BF),
            jax.ShapeDtypeStruct((TAPS * C, C), F32),
        ],
        in_specs=[vmem] * 3,
        out_specs=[anywhere] * 3,
        scratch_shapes=[
            pltpu.VMEM((PARTS, PART_TAPS * C, C), F32),
            pltpu.SemaphoreType.DMA((2 + 4 * PARTS,)),
        ],
        compiler_params=pltpu.CompilerParams(vmem_limit_bytes=48 << 20),
        name="results",
    )(out, dx, codes)


def shards(features, cotangent, coords, orientation, kernel):
    feat = features.reshape(SLOTS, 8, 64, C)
    cot = cotangent.reshape(SLOTS, 8, 64, C)
    out, dx, codes = main_call(coords, orientation, feat, cot, kernel)
    out, dx, total = results(out, dx, codes, float(8 * 64 * 2 * 512) ** -0.5)
    shape = (1, SLOTS, CELLS, C)
    return out.reshape(shape), dx.reshape(shape), total


def solution(mesh):
    in_specs = (
        P("batch", "slab", None, None),
        P("batch", "slab", None, None),
        P("batch", "slab"),
        P("batch"),
        P(),
    )
    out_specs = (P("batch", "slab", None, None), P("batch", "slab", None, None), P())
    return jax.shard_map(shards, mesh=mesh, in_specs=in_specs, out_specs=out_specs, check_vma=False)
```

```python
import functools

import jax
import jax.numpy as jnp
from jax import lax
from jax.experimental import pallas as pl
from jax.experimental.pallas import tpu as pltpu
from jax.sharding import PartitionSpec as P

C = 128
SLOTS = 4
CELLS = 512
TAPS = 27
GROUP = 32
PARTS = 4
PART_TAPS = 7
CHUNK = PART_TAPS * C // 2 // GROUP
ROWS = 16
BITS = 14.95
MIDDLE, LOW, HIGH = list(range(9, 18)), list(range(9)), list(range(18, 27))
ORDER = [list(range(9, 16)), [16, 17, 0, 1, 2, 3, 4], [5, 6, 7, 8, 18, 19, 20], list(range(21, 27))]
BF = jnp.bfloat16
F32 = jnp.float32
MESH = pl.DeviceIdType.MESH


def place():
    s = lax.axis_index("slab")
    return s // 8, (s // 2) & 3, s & 1, lax.axis_index("batch")


def device(z, x, core, y):
    return {"slab": z * 8 + x * 2 + core, "batch": y}


def remote(src, dst, send, recv, where):
    return pltpu.make_async_remote_copy(
        src_ref=src, dst_ref=dst, send_sem=send, recv_sem=recv, device_id=where, device_id_type=MESH
    )


def around(pos):
    row, col = pos >> 2, pos & 3
    inside_y = {-1: row > 0, 0: pos < 16, 1: row < 3}
    inside_x = {-1: col > 0, 0: pos < 16, 1: col < 3}
    return {
        (dy, dx): jnp.where(inside_y[dy] & inside_x[dx] & (pos < 16), pos + 4 * dy + dx, 99)
        for dy in (-1, 0, 1)
        for dx in (-1, 0, 1)
    }


def slots_of(wanted, coord):
    slots = {}
    for offset, position in wanted.items():
        slot = jnp.int32(SLOTS)
        for k in range(SLOTS):
            slot = jnp.where(coord[k] == position, k, slot)
        slots[offset] = slot
    return slots


def build_plane(get, slots, even, odd, i, z):
    lane_x = lax.broadcasted_iota(jnp.int32, (10, 8, C), 1)

    def column(dx):
        middle = get(slots[0, dx], 0, 64).astype(F32).reshape(8, 8, C)
        top = get(slots[-1, dx], 48, 16).astype(F32).reshape(2, 8, C)[1:]
        bottom = get(slots[1, dx], 0, 16).astype(F32).reshape(2, 8, C)[:1]
        return jnp.concatenate([top, middle, bottom], axis=0)

    left, centre, right = column(-1), column(0), column(1)
    before = pltpu.roll(jnp.where(lane_x == 7, left, centre), 1, 1)
    after = pltpu.roll(jnp.where(lane_x == 0, right, centre), 7, 1)
    for d, rows in enumerate((before, centre, after)):
        even[d, i, z] = rows[1:9].reshape(64, C).astype(BF)
        odd[d, i, z] = rows.reshape(80, C).astype(BF)


def shifted(even, odd, tap, brick=None):
    tz, ty, tx = tap // 9, tap // 3 % 3, tap % 3
    which = slice(None) if brick is None else brick
    count = SLOTS if brick is None else 1
    if ty == 1:
        cells = even[tx, which, tz : tz + 8]
    else:
        cells = odd[tx, which, tz : tz + 8, 8 * ty : 8 * ty + 64]
    return cells.reshape(count * CELLS, C)


def encode(rows):
    index = lax.broadcasted_iota(jnp.int32, rows.shape, 1)
    top = jnp.max(jnp.where(index < CHUNK, jnp.abs(rows), 0.0), axis=1, keepdims=True)
    power = jnp.ceil(jnp.log2(jnp.maximum(top, 2.0**-100)))
    codes = jnp.round(rows * jnp.exp2(BITS - power))
    codes = jnp.where(index < CHUNK, codes, jnp.broadcast_to(power, rows.shape))
    return codes.astype(jnp.int32).astype(jnp.int16)


def decode(codes):
    values = codes.astype(jnp.int32).astype(F32)
    return values * jnp.exp2(values[:, CHUNK : CHUNK + 1] - BITS)


def main_kernel(
    coords_in, code_in, feat, cot, kernel, out, dx, gathered,
    coords, code, V, U, HVS, HVO, HU, HCS, HCO, mine_c, near, KV, even_v, odd_v, even_u, odd_u, cot_t, edge_t, terms, grad, sibling,
    out_codes, in_codes, mid_codes, mid_in,
    load_sem, halo_send, halo_recv, core_send, core_recv, s1, r1, s2, r2, s3, r3, hand_send, hand_recv,
):
    slab = lax.axis_index("slab")
    z, x, core, y = place()
    me = (x * 8 + y, x * 8 + z)
    ring_me = (z, y)

    other = device(z, x, 1 - core, y)
    has_lower, has_upper = slab > 0, slab < 63
    lower, upper = {"slab": lax.rem(slab + 63, 64)}, {"slab": lax.rem(slab + 1, 64)}

    near_x = [(x + step) & 3 for step in range(4)]
    near_y, near_z = [(y + step) & 7 for step in range(8)], [(z + step) & 7 for step in range(8)]

    def team(kind):
        for step in (4, 3, 5, 2, 6, 1, 7, 0):
            for step_x in (2, 1, 3, 0):
                if step_x or step:
                    row, column = near_x[step_x], (near_y, near_z)[kind][step]
                    where = device(z, row, core, column) if kind == 0 else device(column, row, core, y)
                    yield row * 8 + column, where

    def ring(kind):
        for step in range(1, 8):
            yield device(near_z[step], x, core, y) if kind == 0 else device(z, x, core, near_y[step])

    loads = [
        pltpu.make_async_copy(feat, V.at[pl.ds(0, SLOTS)], load_sem.at[0]),
        pltpu.make_async_copy(cot, U.at[pl.ds(0, SLOTS)], load_sem.at[1]),
        pltpu.make_async_copy(kernel, KV, load_sem.at[2]),
    ]
    codes = [pltpu.make_async_copy(coords_in, coords, load_sem.at[4]), pltpu.make_async_copy(code_in, code, load_sem.at[5])]
    for load in codes + loads:
        load.start()
    barrier = pltpu.get_barrier_semaphore()
    pl.semaphore_signal(barrier, inc=1, device_id=other, device_id_type=MESH)

    @pl.when(has_upper & (core == 1))
    def _():
        pl.semaphore_signal(barrier, inc=1, device_id=upper, device_id_type=MESH)

    @pl.when(has_lower & (core == 0))
    def _():
        pl.semaphore_signal(barrier, inc=1, device_id=lower, device_id_type=MESH)

    for kind in range(2):
        for _, peer in team(kind):
            pl.semaphore_signal(barrier, inc=1, device_id=peer, device_id_type=MESH)

    for cells in (V, U):
        cells[SLOTS] = jnp.zeros((8, 64, C), BF)
    for planes in (HVS, HVO, HU.at[0], HU.at[1]):
        planes[SLOTS] = jnp.zeros((64, C), BF)
    for z0 in (0, 9):
        even_v[:, :, z0] = jnp.zeros((3, SLOTS, 64, C), BF)
        odd_v[:, :, z0] = jnp.zeros((3, SLOTS, 80, C), BF)
    for copy in codes:
        copy.wait()
    lane = lax.broadcasted_iota(jnp.int32, (8, C), 1)
    row = jnp.full((8, C), 16, jnp.int32)
    for k in range(SLOTS):
        row = jnp.where(lane == k, coords[0, k], row)
    mine_c[...] = row
    for d in range(2):
        for k in range(SLOTS):
            near[d, 0, k] = 16
    flip_code = code[0]
    flip_x, flip_y, flip_z = flip_code & 1, (flip_code >> 1) & 1, (flip_code >> 2) & 1

    def mirrored(tap):
        tz, ty, tx = tap // 9, tap // 3 % 3, tap % 3
        return tap + flip_z * (18 - 18 * tz) + flip_y * (6 - 6 * ty) + flip_x * (2 - 2 * tx)

    def inner(cells, even, odd):
        own = [coords[0, k] for k in range(SLOTS)]

        @pl.loop(0, SLOTS)
        def _(i):
            slots = slots_of(around(coords[0, i]), own)

            @pl.loop(0, 8)
            def _(plane):
                build_plane(lambda j, a, n: cells[j, plane, pl.ds(a, n), :], slots, even, odd, i, plane + 1)

    def outer(planes, even, odd, n, d, there):
        theirs = [jnp.where(there, near[n, 0, k], 16) for k in range(SLOTS)]

        @pl.loop(0, SLOTS)
        def _(i):
            slots = slots_of(around(coords[0, i]), theirs)
            build_plane(lambda j, a, m: planes[j, pl.ds(a, m), :], slots, even, odd, i, 9 * d)

    loads[0].wait()
    inner(V, even_v, odd_v)
    loads[1].wait()
    zero = jnp.zeros((), BF)
    for i in range(SLOTS):
        cells = jnp.where(coords[0, i] < 16, U[i].reshape(CELLS, C), zero)
        cot_t[:, i * CELLS : (i + 1) * CELLS] = cells.T
    for d, plane in ((0, 0), (1, 7)):
        edge = [jnp.where(coords[0, i] < 16, U[i, plane], zero) for i in range(SLOTS)]
        edge_t[d] = jnp.concatenate(edge, axis=0).T
    def products(taps, left, read):
        for first in range(0, len(taps), 2):
            two = taps[first : first + 2]
            cols = jnp.concatenate([read(t) for t in two], axis=1)
            sums = jnp.dot(left, cols, preferred_element_type=F32)
            for k, t in enumerate(two):
                yield t, sums[:, k * C : (k + 1) * C].T

    def fill(part):
        for n, t in enumerate(ORDER[part]):
            grad[part, n * C : (n + 1) * C] = terms[mirrored(t)]

    def own_terms(taps):
        for t, term in products(taps, cot_t[...], lambda t: shifted(even_v, odd_v, t)):
            terms[t] = term

    own_terms(MIDDLE)
    fill(0)

    half = PART_TAPS * C // 2

    def to_core(part):
        src = grad.at[part, pl.ds(pl.multiple_of((1 - core) * half, 8), half)]
        return remote(src, sibling.at[part, pl.ds(0, half)], core_send.at[part], core_recv.at[part], other)

    pl.semaphore_wait(barrier, 2 * GROUP - 1 + ((has_upper & (core == 1)) | (has_lower & (core == 0))).astype(jnp.int32))

    has_outer = jnp.where(core == 0, has_lower, has_upper)
    beyond = {"slab": lax.rem(slab + 63 + 2 * core, 64)}
    halos = []
    for n, (peer, plane, c_land, v_land) in enumerate(((other, 7 * (1 - core), HCS, HVS), (beyond, 7 * core, HCO, HVO))):
        halos.append(
            [
                remote(mine_c, c_land, halo_send.at[n, 0], halo_recv.at[n, 0], peer),
                remote(V.at[pl.ds(0, SLOTS), plane], v_land.at[pl.ds(0, SLOTS)], halo_send.at[n, 1], halo_recv.at[n, 1], peer),
                remote(U.at[pl.ds(0, SLOTS), plane], HU.at[n, pl.ds(0, SLOTS)], halo_send.at[n, 2], halo_recv.at[n, 2], peer),
            ]
        )

    def start_halo(k):
        pl.when(has_outer)(halos[1][k].start)
        halos[0][k].start()

    start_halo(0)
    start_halo(1)
    to_core(0).start()
    start_halo(2)

    def scatter(part):
        landing = in_codes.at[part, me[part % 2]]
        for j, peer in team(part % 2):
            remote(out_codes.at[part, j], landing, s1.at[part], r1.at[part], peer).start()

    def send_part(part):
        to_core(part).wait_recv()

        @pl.loop(0, GROUP // 8)
        def _(eight):
            base = pl.multiple_of(eight * 8 * CHUNK, 8)
            mine = grad[part, pl.ds(pl.multiple_of(core * half + base, 8), 120)]
            rows = mine + sibling[part, pl.ds(base, 120)]
            blocks = jnp.stack([rows[n * CHUNK : n * CHUNK + ROWS] for n in range(8)])
            out_codes[part, pl.ds(eight * 8, 8)] = encode(blocks)

        scatter(part)

    own_terms(LOW + HIGH)
    for n in range(len(ORDER[PARTS - 1]), PART_TAPS):
        grad[PARTS - 1, n * C : (n + 1) * C] = jnp.zeros((C, C), F32)
    send_part(0)
    inner(U, even_u, odd_u)

    for n, (d, there) in enumerate(((1 - core, True), (core, has_outer))):
        near_copy = pltpu.make_async_copy((HCS, HCO)[n], near.at[n], load_sem.at[3])

        def arrived(n=n, near_copy=near_copy):
            halos[n][0].wait_recv()
            near_copy.start()
            halos[n][1].wait_recv()
            near_copy.wait()

        if n == 0:
            arrived()
        else:
            pl.when(there)(arrived)
        outer((HVS, HVO)[n], even_v, odd_v, n, d, there)

        def edge_cells(t, d=d):
            ty, tx = t // 3, t % 3
            if ty == 1:
                return even_v[tx, :, 9 * d].reshape(SLOTS * 64, C)
            return odd_v[tx, :, 9 * d, 8 * ty : 8 * ty + 64].reshape(SLOTS * 64, C)

        for t, term in products(LOW, edge_t[d], edge_cells):
            terms[t + 18 * d] += term
    for part in range(1, PARTS):
        fill(part)
        to_core(part).start()
    for part in range(1, PARTS):
        send_part(part)

    def convolve(i, backward):
        total = jnp.zeros((CELLS, C), F32)
        for first in range(0, TAPS, 2):
            taps = range(first, min(first + 2, TAPS))
            if backward:
                cols = jnp.concatenate([shifted(even_u, odd_u, 26 - t, i) for t in taps], axis=1)
                weights = jnp.concatenate([KV[mirrored(t)] for t in taps], axis=1)
                dims = (((1,), (1,)), ((), ()))
            else:
                cols = jnp.concatenate([shifted(even_v, odd_v, t, i) for t in taps], axis=1)
                weights = jnp.concatenate([KV[mirrored(t)] for t in taps], axis=0)
                dims = (((1,), (0,)), ((), ()))
            total += lax.dot_general(cols, weights, dims, preferred_element_type=F32)
        return jnp.where(coords[0, i] < 16, total, 0.0).astype(BF).reshape(8, 64, C)

    loads[2].wait()

    @pl.loop(0, SLOTS)
    def _(i):
        out[i] = convolve(i, False)

    halos[0][2].wait_recv()
    pl.when(has_outer)(halos[1][2].wait_recv)
    outer(HU.at[0], even_u, odd_u, 0, 1 - core, True)
    outer(HU.at[1], even_u, odd_u, 1, core, has_outer)

    def exchange(part):
        landing = mid_in.at[part, ring_me[part % 2]]
        for peer in ring(part % 2):
            remote(mid_codes.at[part], landing, s2.at[part], r2.at[part], peer).start()

    def several(buffer, count, send, recv):
        blocks = buffer.at[pl.ds(0, count)]
        return remote(blocks, blocks, send, recv, other)

    for part in range(PARTS):
        kind = part % 2
        several(in_codes.at[part], GROUP - 1, s1.at[part], r1.at[part]).wait_recv()

        in_codes[part, me[kind]] = out_codes[part, me[kind]]

        def add(eight, total):
            return total + jnp.sum(decode(in_codes[part, pl.ds(eight * 8, 8)]), axis=0, keepdims=True)

        total = lax.fori_loop(0, GROUP // 8, add, jnp.zeros((1, ROWS, C), F32))
        codes = encode(total)[0]
        mid_codes[part] = codes
        mid_in[part, ring_me[kind]] = codes

        exchange(part)

    @pl.loop(0, 1)
    def _(i):
        dx[i] = convolve(i, True)

    def publish(part):
        block = gathered.at[part, core, me[part % 2]]
        for _, peer in team(part % 2):
            remote(block, block, s3.at[part], r3.at[part], peer).start()

    for part in range(PARTS):
        kind = part % 2
        several(mid_in.at[part], 7, s2.at[part], r2.at[part]).wait_recv()
        total = jnp.sum(decode(mid_in[part]), axis=0, keepdims=True)
        gathered[part, core, me[kind]] = encode(total)[0]

        publish(part)

    @pl.loop(1, SLOTS)
    def _(i):
        dx[i] = convolve(i, True)

    def hand(part):
        block = gathered.at[part, core]
        return remote(block, block, hand_send.at[part], hand_recv.at[part], other)

    for part in range(PARTS):
        several(gathered.at[part, core], GROUP - 1, s3.at[part], r3.at[part]).wait_recv()
        hand(part).start()

    for part in range(PARTS):
        to_core(part).wait_send()
        several(out_codes.at[part], GROUP - 1, s1.at[part], r1.at[part]).wait_send()
        several(mid_in.at[part], 7, s2.at[part], r2.at[part]).wait_send()
        several(gathered.at[part, core], GROUP - 1, s3.at[part], r3.at[part]).wait_send()
        hand(part).wait_send()
    for copy in halos[0]:
        copy.wait_send()
    for copy in halos[1]:
        pl.when(has_outer)(copy.wait_send)
    for part in range(PARTS):
        hand(part).wait_recv()


def main_call(coords, code, feat, cot, kernel):
    vmem = pl.BlockSpec(memory_space=pltpu.VMEM)
    anywhere = pl.BlockSpec(memory_space=pl.ANY)
    dma = pltpu.SemaphoreType.DMA
    cells, planes = pltpu.VMEM((SLOTS + 1, 8, 64, C), BF), pltpu.VMEM((2, SLOTS + 1, 64, C), BF)
    side, row = pltpu.VMEM((SLOTS + 1, 64, C), BF), pltpu.VMEM((8, C), jnp.int32)
    even, odd = pltpu.VMEM((3, SLOTS, 10, 64, C), BF), pltpu.VMEM((3, SLOTS, 10, 80, C), BF)
    codes = pltpu.VMEM((PARTS, GROUP, ROWS, C), jnp.int16)
    return pl.pallas_call(
        main_kernel,
        out_shape=[
            pltpu.VMEM((SLOTS, 8, 64, C), BF),
            pltpu.VMEM((SLOTS, 8, 64, C), BF),
            pltpu.VMEM((PARTS, 2, GROUP, ROWS, C), jnp.int16),
        ],
        in_specs=[anywhere] * 5,
        out_specs=[vmem] * 3,
        scratch_shapes=[
            pltpu.SMEM((1, SLOTS), jnp.int32), pltpu.SMEM((1,), jnp.int32), cells, cells, side, side, planes, row, row, row,
            pltpu.SMEM((2, 8, C), jnp.int32), pltpu.VMEM((TAPS, C, C), BF), even, odd, even, odd,
            pltpu.VMEM((C, SLOTS * CELLS), BF), pltpu.VMEM((2, C, SLOTS * 64), BF), pltpu.VMEM((TAPS, C, C), F32),
            pltpu.VMEM((PARTS, PART_TAPS * C + 8, C), F32), pltpu.VMEM((PARTS, PART_TAPS * C // 2 + 8, C), F32),
            codes, codes, pltpu.VMEM((PARTS, ROWS, C), jnp.int16), pltpu.VMEM((PARTS, 8, ROWS, C), jnp.int16),
            dma((6,)), dma((2, 3)), dma((2, 3)), dma((PARTS,)), dma((PARTS,)), dma((PARTS,)), dma((PARTS,)),
            dma((PARTS,)), dma((PARTS,)), dma((PARTS,)), dma((PARTS,)), dma((PARTS,)), dma((PARTS,)),
        ],
        compiler_params=pltpu.CompilerParams(collective_id=0, has_side_effects=True, vmem_limit_bytes=60 << 20),
        name="brick_convs",
    )(coords, code, feat, cot, kernel)


def result_kernel(scale, out_in, dx_in, codes, out, dx, grad, rows, sems):
    copies = [pltpu.make_async_copy(out_in, out, sems.at[0]), pltpu.make_async_copy(dx_in, dx, sems.at[1])]
    for copy in copies:
        copy.start()
    half = PART_TAPS * C // 2
    stores = []
    for part in range(PARTS):
        for core in range(2):

            @pl.loop(0, GROUP // 8)
            def _(eight):
                blocks = decode(codes[part, core, pl.ds(eight * 8, 8)]) * scale
                start = pl.multiple_of(core * half + eight * 8 * CHUNK, 8)
                rows[part, pl.ds(start, 8 * CHUNK)] = jnp.concatenate([blocks[n, :CHUNK] for n in range(8)], axis=0)

        first = 0
        taps = ORDER[part]
        for n in range(1, len(taps) + 1):
            if n == len(taps) or taps[n] != taps[n - 1] + 1:
                store = pltpu.make_async_copy(
                    rows.at[part, pl.ds(first * C, (n - first) * C)],
                    grad.at[pl.ds(taps[first] * C, (n - first) * C)],
                    sems.at[2 + len(stores)],
                )
                store.start()
                stores.append(store)
                first = n
    for copy in stores + copies:
        copy.wait()


def results(out, dx, codes, scale):
    anywhere, vmem = pl.BlockSpec(memory_space=pl.ANY), pl.BlockSpec(memory_space=pltpu.VMEM)
    return pl.pallas_call(
        functools.partial(result_kernel, scale),
        out_shape=[
            jax.ShapeDtypeStruct((SLOTS, 8, 64, C), BF),
            jax.ShapeDtypeStruct((SLOTS, 8, 64, C), BF),
            jax.ShapeDtypeStruct((TAPS * C, C), F32),
        ],
        in_specs=[vmem] * 3,
        out_specs=[anywhere] * 3,
        scratch_shapes=[
            pltpu.VMEM((PARTS, PART_TAPS * C, C), F32),
            pltpu.SemaphoreType.DMA((2 + 4 * PARTS,)),
        ],
        compiler_params=pltpu.CompilerParams(vmem_limit_bytes=48 << 20),
        name="results",
    )(out, dx, codes)


def shards(features, cotangent, coords, orientation, kernel):
    feat = features.reshape(SLOTS, 8, 64, C)
    cot = cotangent.reshape(SLOTS, 8, 64, C)
    out, dx, codes = main_call(coords, orientation, feat, cot, kernel)
    out, dx, total = results(out, dx, codes, float(8 * 64 * 2 * 512) ** -0.5)
    shape = (1, SLOTS, CELLS, C)
    return out.reshape(shape), dx.reshape(shape), total


def solution(mesh):
    in_specs = (
        P("batch", "slab", None, None),
        P("batch", "slab", None, None),
        P("batch", "slab"),
        P("batch"),
        P(),
    )
    out_specs = (P("batch", "slab", None, None), P("batch", "slab", None, None), P())
    return jax.shard_map(shards, mesh=mesh, in_specs=in_specs, out_specs=out_specs, check_vma=False)
```
